256 devices in a mesh: group: 8 (over y, core), dev: 32 (over z, x).
Axes of the slice: x: 4, y: 4, z: 8, core: 2. Of those that a mesh axis runs over, the one named last changes fastest.
Arguments:
- node_feats: bfloat16 [262144, 512], P(('group', 'dev')), may hold values from -6 to 6
- aggregate: bfloat16 [262144, 512], P(('group', 'dev')), may hold values from -6 to 6
- cotangent: bfloat16 [262144, 512], P(('group', 'dev')), may hold values from -6 to 6
- msg_weight: bfloat16 [512, 512], P('dev'), may hold values from -0.25 to 0.25
- upd_weight: bfloat16 [512, 512], P('dev'), may hold values from -0.25 to 0.25
- self_weight: bfloat16 [512, 512], P('dev'), may hold values from -0.25 to 0.25
- owner_map: int32 [8, 256], P('group'), may hold values from 0 to 255, as said below
- inner_source: int32 [16384], P(('group', 'dev')), may hold values from 0 to 255, as said below
- inner_target: int32 [16384], P(('group', 'dev')), may hold values from 0 to 7
- inner_contact: bfloat16 [16384, 128, 128], P(('group', 'dev')), may hold values from -0.1796875 to 0.1796875
- send_counts: int32 [256, 32], P(('group', 'dev')), may hold values from 1 to 2, as said below
- halo_source: int32 [16384], P(('group', 'dev')), may hold values from 0 to 7
- halo_target: int32 [16384], P(('group', 'dev')), may hold values from 0 to 7
- halo_contact: bfloat16 [16384, 128, 128], P(('group', 'dev')), may hold values from -0.1796875 to 0.1796875
Outputs:
- grad_nodes: bfloat16 [262144, 512], P(('group', 'dev'))
- grad_msg: float32 [512, 512], P('dev')
- grad_upd: float32 [512, 512], P('dev')
- grad_self: float32 [512, 512], P('dev')
The draws below stay inside these ranges and needn't reach their ends.
Inputs may be any that keep to these rules, and one draw needn't show every extreme that they name: Each row is a permutation: block b of slab g is stored at slot owner_map[g, b], on device slot // 8 of the slab, local block slot % 8. `inner_source`: the slots of device k for peer p name blocks stored on device p of k's slab. `send_counts`: every device has at least one live slot for every peer; in every draw one peer column is 2 on every device.
All inputs are finite; a program needn't handle non-finite values.
Results may differ from the reference program's by a relative error of at most 0.0095.
Values may be sent and summed in bfloat16 or wider, within the bound.
A program may use at most 128 MiB of HBM per device.

```python
import math
import jax
import jax.numpy as jnp
from jax import lax

D = 512
BLK = 128
B_DEV = 8
CAP = 2
H_DEV = 64
NB = 256
SLOTS = 64
NODES = 262144
N_GROUP = 8
N_DEV = 32


def owner_table(key):
    group_keys = jax.random.split(key, N_GROUP)
    return jax.vmap(lambda one_key: jax.random.permutation(one_key, NB))(group_keys).astype(jnp.int32)


def draw_owner_map(key, part):
    owner_rows = owner_table(key)
    return owner_rows


def draw_inner_source(key, part):
    owner_rows = owner_table(key)
    key = jax.random.fold_in(key, 12)
    inverse = jnp.argsort(owner_rows, axis=1, stable=True).astype(jnp.int32)
    local_pick = jax.random.randint(key, (N_GROUP, N_DEV, N_DEV, CAP), 0, B_DEV, dtype=jnp.int32)
    peer_ids = jnp.arange(N_DEV, dtype=jnp.int32)[None, None, :, None]
    slot_ids = peer_ids * B_DEV + local_pick
    chosen = jax.vmap(lambda owner_row, picked: owner_row[picked])(inverse, slot_ids)
    return chosen.reshape(N_GROUP * N_DEV * N_DEV * CAP).astype(jnp.int32)


def draw_send_counts(key, part):
    key = jax.random.fold_in(key, 13)
    counts = jax.random.randint(key, (N_GROUP * N_DEV, N_DEV), 1, CAP + 1, dtype=jnp.int32)
    full_peer = jax.random.randint(jax.random.fold_in(key, 5), (), 0, N_DEV, dtype=jnp.int32)
    column_ids = jnp.arange(N_DEV, dtype=jnp.int32)[None, :]
    return jnp.where(column_ids == full_peer, CAP, counts).astype(jnp.int32)


def touch_ends(drawn, stream_key, low, top_value):
    longest = drawn.shape.index(max(drawn.shape))
    spots = []
    for shift in (0, 1):
        where = [jax.random.randint(jax.random.fold_in(stream_key, axis), (), 0, length) for axis, length in enumerate(drawn.shape)]
        where[longest] = (where[longest] + shift) % drawn.shape[longest]
        spots.append(tuple(where))
    return drawn.at[spots[0]].set(low).at[spots[1]].set(top_value)


def shard_levels(stream_key, shape, cuts, least, largest):
    def one(dim, shards_of):
        heights = jax.random.uniform(jax.random.fold_in(jax.random.fold_in(stream_key, 6), dim), (shards_of,), jnp.float32, least / len(cuts), largest / len(cuts))
        return jnp.repeat(jnp.exp(heights), shape[dim] // shards_of).reshape((-1,) + (1,) * (len(shape) - dim - 1))

    level = one(*cuts[0])
    for cut in cuts[1:]:
        level = level * one(*cut)
    return level


def gaussian(rng, dims, spread, most, shards=(), kind=jnp.bfloat16):
    result = spread * jax.random.normal(rng, dims, jnp.float32)
    if shards:
        result = result * shard_levels(rng, dims, shards, -0.22, 0.18)
    return jnp.clip(result, -most, most).astype(kind)


def setup_inputs(seed: int = 0) -> dict:
    arg_keys = jax.random.split(jax.random.key(seed), 15)
    node_feats = gaussian(arg_keys[0], (NODES, D), 1.0, 6.0, ((0, 256),))
    aggregate = gaussian(arg_keys[1], (NODES, D), 1.0, 6.0, ((0, 256),))
    cotangent = gaussian(arg_keys[2], (NODES, D), 1.0, 6.0, ((0, 256),))
    msg_weight = gaussian(arg_keys[3], (D, D), D ** -0.5, 0.25, ((0, 32),))
    upd_weight = gaussian(arg_keys[4], (D, D), D ** -0.5, 0.25, ((0, 32),))
    self_weight = gaussian(arg_keys[5], (D, D), D ** -0.5, 0.25, ((0, 32),))
    owner_map = draw_owner_map(jax.random.fold_in(arg_keys[14], 71), 0)
    inner_source = draw_inner_source(jax.random.fold_in(arg_keys[14], 71), 0)
    inner_target = touch_ends(jax.random.randint(arg_keys[8], (N_GROUP * N_DEV * SLOTS,), 0, B_DEV), jax.random.fold_in(arg_keys[8], 1), 0, B_DEV - 1).astype(jnp.int32)
    inner_contact = gaussian(arg_keys[9], (N_GROUP * N_DEV * SLOTS, BLK, BLK), 0.03, 0.1796875, ((0, 256),))
    send_counts = draw_send_counts(jax.random.fold_in(arg_keys[14], 71), 0)
    halo_source = touch_ends(jax.random.randint(arg_keys[11], (N_GROUP * N_DEV * H_DEV,), 0, B_DEV), jax.random.fold_in(arg_keys[11], 1), 0, B_DEV - 1).astype(jnp.int32)
    halo_target = touch_ends(jax.random.randint(arg_keys[12], (N_GROUP * N_DEV * H_DEV,), 0, B_DEV), jax.random.fold_in(arg_keys[12], 1), 0, B_DEV - 1).astype(jnp.int32)
    halo_contact = gaussian(arg_keys[13], (N_GROUP * N_DEV * H_DEV, BLK, BLK), 0.03, 0.1796875, ((0, 256),))
    return dict(node_feats=node_feats, aggregate=aggregate, cotangent=cotangent, msg_weight=msg_weight, upd_weight=upd_weight, self_weight=self_weight, owner_map=owner_map, inner_source=inner_source, inner_target=inner_target, inner_contact=inner_contact, send_counts=send_counts, halo_source=halo_source, halo_target=halo_target, halo_contact=halo_contact)


def reference(node_feats, aggregate, cotangent, msg_weight, upd_weight, self_weight, owner_map, inner_source, inner_target, inner_contact, send_counts, halo_source, halo_target, halo_contact):
    device_count = N_GROUP * N_DEV
    slot_count = N_DEV * CAP
    slab_blocks = B_DEV * N_DEV
    block_total = device_count * B_DEV
    pre_act = jnp.dot(aggregate, upd_weight, preferred_element_type=jnp.float32) + jnp.dot(node_feats, self_weight, preferred_element_type=jnp.float32)
    sigmoid_z = jax.nn.sigmoid(pre_act)
    grad_pre = (cotangent.astype(jnp.float32) * sigmoid_z * (1.0 + pre_act * (1.0 - sigmoid_z))).astype(jnp.bfloat16)
    grad_agg = jnp.dot(grad_pre, upd_weight.T, preferred_element_type=jnp.float32).astype(jnp.bfloat16)
    agg_blocks = grad_agg.reshape(block_total, BLK, D)
    slot_ids = jnp.arange(slot_count, dtype=jnp.int32)

    def one_device(summed, packed):
        device_id, inner_targets, inner_sources, inner_blocks, slot_counts, halo_targets, halo_sources, halo_blocks = packed
        group_id = device_id // N_DEV
        column_id = device_id % N_DEV
        live_slots = slot_ids % CAP < slot_counts[slot_ids // CAP]
        gathered = agg_blocks[device_id * B_DEV + inner_targets]
        edge_grads = jnp.einsum('pij,pid->pjd', inner_blocks.astype(jnp.float32), gathered.astype(jnp.float32))
        edge_grads = jnp.where(live_slots[:, None, None], edge_grads, 0.0).astype(jnp.bfloat16)
        edge_grads = lax.optimization_barrier(edge_grads).astype(jnp.float32)
        sources = group_id * slab_blocks + owner_map[group_id][inner_sources]
        summed = summed.at[sources].add(edge_grads)
        halo_rows = agg_blocks[device_id * B_DEV + halo_targets]
        halo_grads = jnp.einsum('pij,pid->pjd', halo_blocks.astype(jnp.float32), halo_rows.astype(jnp.float32)).astype(jnp.bfloat16)
        halo_grads = lax.optimization_barrier(halo_grads).astype(jnp.float32)
        keep_halo = group_id < N_GROUP - 1
        halo_dest = jnp.minimum(((group_id + 1) * N_DEV + column_id) * B_DEV + halo_sources, block_total - 1)
        summed = summed.at[halo_dest].add(jnp.where(keep_halo, halo_grads, 0.0))
        return (summed, None)
    packed = (jnp.arange(device_count, dtype=jnp.int32), inner_target.reshape(device_count, slot_count), inner_source.reshape(device_count, slot_count), inner_contact.reshape(device_count, slot_count, BLK, BLK), send_counts, halo_target.reshape(device_count, H_DEV), halo_source.reshape(device_count, H_DEV), halo_contact.reshape(device_count, H_DEV, BLK, BLK))
    summed, unused = lax.scan(one_device, jnp.zeros((block_total, BLK, D), jnp.float32), packed)
    msg_grad = summed.reshape(block_total * BLK, D).astype(jnp.bfloat16)
    grad_nodes = (cotangent.astype(jnp.float32) + jnp.dot(grad_pre, self_weight.T, preferred_element_type=jnp.float32) + jnp.dot(msg_grad, msg_weight.T, preferred_element_type=jnp.float32)).astype(jnp.bfloat16)
    grad_scale = 1.0 / math.sqrt(block_total * BLK)
    grad_msg = jnp.dot(node_feats.T, msg_grad, preferred_element_type=jnp.float32) * grad_scale
    grad_upd = jnp.dot(aggregate.T, grad_pre, preferred_element_type=jnp.float32) * grad_scale
    grad_self = jnp.dot(node_feats.T, grad_pre, preferred_element_type=jnp.float32) * grad_scale
    return (grad_nodes, grad_msg, grad_upd, grad_self)
```

```python
import math

import jax
import jax.numpy as jnp
from jax import lax
from jax.experimental import pallas as pl
from jax.experimental.pallas import tpu as pltpu
from jax.sharding import PartitionSpec as P

BF = jnp.bfloat16
F32 = jnp.float32
NX = 4
LANES = 128
MESH = pl.DeviceIdType.MESH


def dot(a, b, ca, cb):
    return lax.dot_general(a, b, (((ca,), (cb,)), ((), ())), preferred_element_type=F32)


def make_kernel(NG, ND, R, D, NB, CAP, NH, scale):
    NZ = ND // NX
    NY = NG // 2
    ZZ = NZ // NY
    NCH = D // LANES
    NSL = NX * CAP
    HALF = NZ // 2
    TR = min(256, R)
    NI = 2 * NCH
    TL = ZZ * NX
    ZROW = NX * 16

    def kernel(*refs):
        names = [
            "nf_h", "agg_h", "cot_h", "msg_h", "upd_h", "self_h", "own_s", "meta_v", "hsrc_s", "htgt_s",
            "inner_h", "halo_h", "gn_o", "gw_o",
        ] + [n for n, _ in scratch]
        r = dict(zip(names, refs))
        gall = [r["g%d" % c] for c in range(NCH)]
        g = lax.axis_index("group")
        d = lax.axis_index("dev")
        y, h = g // 2, g % 2
        z, x = d // NX, d % NX
        sib = y * 2 + (1 - h)

        def xdev(k):
            return z * NX + (x + k) % NX

        def zdev(k):
            return ((z + k + NZ) % NZ) * NX + x

        def rc(src, dst, ss, rs, gg, dd):
            return pltpu.make_async_remote_copy(
                src_ref=src, dst_ref=dst, send_sem=ss, recv_sem=rs, device_id=(gg, dd), device_id_type=MESH
            )

        pending = []

        def send(src, dst, ss, rs, gg, dd):
            cp = rc(src, dst, ss, rs, gg, dd)
            cp.start()
            pending.append(cp)

        def got(dst, rs):
            rc(dst, dst, rs, rs, sib, d).wait_recv()

        loads = {}

        def load(name, src, dst, i):
            cp = pltpu.make_async_copy(src, dst, r["lsem"].at[i])
            cp.start()
            loads[name] = cp

        HD = D // 2
        load("upd", r["upd_h"], r["wst"].at[0], 0)
        load("self", r["self_h"], r["wst"].at[1], 1)
        load("m0", r["msg_h"].at[:, pl.ds(0, HD)], r["mst"].at[0], 2)
        load("m1", r["msg_h"].at[:, pl.ds(HD, HD)], r["mst"].at[1], 3)

        bar = pltpu.get_barrier_semaphore()

        def greet(gg, dd):
            pl.semaphore_signal(bar, inc=1, device_id=(gg, dd), device_id_type=MESH)

        for k in range(1, NX):
            greet(g, xdev(k))
        for k in range(1, NZ):
            greet(g, zdev(k))
        for k in range(1, NG):
            greet((g + k) % NG, d)
        zero = jnp.zeros((LANES, LANES), F32)
        r["ebuf"][NSL] = zero
        r["hbuf"][NH] = zero
        for c in range(NCH):
            gall[c][NX * NB] = zero.astype(BF)
        for n in ("upd", "self", "m0", "m1"):
            loads[n].wait()
        W, M = r["W"], r["M"]
        row0 = pl.multiple_of(d * 16, 16)
        plane = pl.ds(pl.multiple_of(z * ZROW, 16), ZROW)
        W[h, pl.ds(row0, 16), :] = r["wst"][h]
        M[h, pl.ds(row0, 16), :] = r["mst"][h]
        r["mrecv"][x] = r["meta_v"][x]
        pl.semaphore_wait(bar, NX - 1 + NZ - 1 + NG - 1)

        myrow = pl.ds(row0, 16)
        for k in (1, 3, 2):
            send(r["wst"].at[h], W.at[h, myrow], r["w1s"].at[k], r["w1r"].at[k], g, xdev(k))
        for k in (1, 3, 2):
            send(r["mst"].at[h], M.at[h, myrow], r["m1s"].at[k], r["m1r"].at[k], g, xdev(k))
            send(r["meta_v"].at[(x + k) % NX], r["mrecv"].at[x], r["mts"].at[k], r["mtr"].at[k], g, xdev(k))
        load("agg", r["agg_h"], r["agg"], 0)
        load("nf", r["nf_h"], r["nf"], 1)
        load("cot", r["cot_h"], r["cot"], 2)
        load("halo", r["halo_h"], r["chalo"], 3)
        load("cin", r["inner_h"].at[:, x], r["cin"].at[x], 4)
        for k in (1, 3, 2):
            got(W.at[h, myrow], r["w1r"].at[k])
        for k in range(1, NZ):
            send(W.at[h, plane], W.at[h, plane], r["w2s"].at[k], r["w2r"].at[k], g, zdev(k))
        send(W.at[h, plane], W.at[h, plane], r["w3s"].at[0], r["w3r"].at[0], sib, d)
        for k in (1, 3, 2):
            send(r["inner_h"].at[:, (x + k) % NX], r["cin"].at[x], r["cs"].at[k], r["cr"].at[k], g, xdev(k))
        for k in (1, 3, 2):
            got(M.at[h, myrow], r["m1r"].at[k])
            got(r["mrecv"].at[x], r["mtr"].at[k])
        cp = pltpu.make_async_copy(r["mrecv"], r["msm"], r["lsem"].at[5])
        cp.start()

        def hstep(s, last):
            src = r["hsrc_s"][s]
            prev = jnp.int32(NH)
            for b in range(NB):
                prev = jnp.where(src == b, last[b], prev)
            r["hidx"][s] = prev
            return tuple(jnp.where(src == b, s, last[b]) for b in range(NB))

        last = lax.fori_loop(0, NH, hstep, (jnp.int32(NH),) * NB)
        for b in range(NB):
            r["hidx"][NH + b] = last[b]
        cp.wait()

        def istep(zt, carry):
            dst = []
            for s in range(NSL):
                xs, cc = s // CAP, s % CAP
                dst.append(lax.rem(r["own_s"][0, r["msm"][xs, zt, cc]], NB))
                r["idx"][zt, s] = jnp.where(
                    cc < r["msm"][xs, zt, 2 * CAP], xs * NB + r["msm"][xs, zt, CAP + cc], NX * NB
                )
            for s in range(NSL):
                p = jnp.int32(NSL)
                for j in range(s):
                    p = jnp.where(dst[j] == dst[s], j, p)
                r["idx"][zt, NSL + s] = p
            for b in range(NB):
                p = jnp.int32(NSL)
                for j in range(NSL):
                    p = jnp.where(dst[j] == b, j, p)
                r["idx"][zt, 2 * NSL + b] = p
            return carry

        lax.fori_loop(0, NZ, istep, 0)

        zorder = sorted(range(1, NZ), key=lambda k: min(k, NZ - k))

        def zplane(k):
            return pl.ds(pl.multiple_of(((z - k + NZ) % NZ) * ZROW, 16), ZROW)

        for k in zorder:
            got(W.at[h, zplane(k)], r["w2r"].at[k])
            send(W.at[h, zplane(k)], W.at[h, zplane(k)], r["w3s"].at[k], r["w3r"].at[k], sib, d)
        for k in range(1, NZ):
            send(M.at[h, plane], M.at[h, plane], r["m2s"].at[k], r["m2r"].at[k], g, zdev(k))
        send(M.at[h, plane], M.at[h, plane], r["m3s"].at[0], r["m3r"].at[0], sib, d)
        for k in [0] + zorder:
            got(W.at[1 - h, zplane(k)], r["w3r"].at[k])
        for n in ("agg", "nf", "cot", "halo", "cin"):
            loads[n].wait()

        def pstep(i, carry):
            rows = pl.ds(pl.multiple_of(i * TR, TR), TR)
            pre = dot(r["agg"][rows, :], W[0], 1, 0) + dot(r["nf"][rows, :], W[1], 1, 0)
            sg = jax.nn.sigmoid(pre)
            gp = (r["cot"][rows, :].astype(F32) * sg * (1.0 + pre * (1.0 - sg))).astype(BF)
            r["gp"][rows, :] = gp
            gt = dot(W[0], gp, 1, 1).astype(BF)
            for t in range(TR // LANES):
                for c in range(NCH):
                    tile = gt[c * LANES : (c + 1) * LANES, t * LANES : (t + 1) * LANES]
                    r["gown"][c, i * (TR // LANES) + t] = tile
                    gall[c][x * NB + i * (TR // LANES) + t] = tile
            return carry

        lax.fori_loop(0, R // TR, pstep, 0)

        NHB = NB // 2

        def xsend(c):
            for k in (1, 3):
                send(
                    r["gown"].at[c], gall[c].at[pl.ds(x * NB, NB)], r["gs"].at[c, k], r["gr"].at[c, k], g, xdev(k)
                )

        def xforward(c):
            for k, off in ((1, 0), (3, NHB)):
                xs = (x - k + NX) % NX
                got(gall[c].at[pl.ds(xs * NB, NB)], r["gr"].at[c, k])
                part = gall[c].at[pl.ds(xs * NB + off, NHB)]
                send(part, part, r["gs"].at[c, 4 + k], r["gr"].at[c, 4 + k], g, xdev(k))

        def xlast(c):
            xs = (x + 2) % NX
            for k, off in ((1, 0), (3, NHB)):
                got(gall[c].at[pl.ds(xs * NB + off, NHB)], r["gr"].at[c, 4 + k])

        def halo(c):
            def step(i, carry):
                for j in range(8):
                    s = i * 8 + j
                    r["hbuf"][s] = dot(r["gown"][c, r["htgt_s"][s]], r["chalo"][s], 1, 0)
                for j in range(8):
                    s = i * 8 + j
                    r["hbuf"][s] = r["hbuf"][s] + r["hbuf"][r["hidx"][s]]
                return carry

            lax.fori_loop(0, NH // 8, step, 0)
            for b in range(NB):
                r["hsend"][c, b] = r["hbuf"][r["hidx"][NH + b]].astype(BF)

        ring = r["ring"]

        def partial(c, zt):
            for s in range(NSL):
                r["ebuf"][s] = dot(gall[c][r["idx"][zt, s]], r["cin"][s // CAP, zt, s % CAP], 1, 0)
            for s in range(1, NSL):
                r["ebuf"][s] = r["ebuf"][s] + r["ebuf"][r["idx"][zt, NSL + s]]

        def summed(zt, b):
            return r["ebuf"][r["idx"][zt, 2 * NSL + b]]

        def ring_step(c, q, dr, has_recv):
            dd = HALF - q
            sgn = 1 - 2 * dr
            zt = (z + sgn * dd + NZ) % NZ
            partial(c, zt)
            slot = ring.at[dr, c, q]
            if has_recv:
                got(slot, r["rr"].at[dr, c, q])
                for b in range(NB):
                    ring[dr, c, q, b] = (summed(zt, b) + ring[dr, c, q, b].astype(F32)).astype(BF)
            else:
                for b in range(NB):
                    ring[dr, c, q, b] = summed(zt, b).astype(BF)
            nz = ((z + sgn + NZ) % NZ) * NX + x
            cp = rc(slot, ring.at[dr, c, q + 1], r["rs"].at[dr, c, q], r["rr"].at[dr, c, q + 1], g, nz)
            cp.start()
            pending.append(cp)

        class Reduce:
            def __init__(self, n, c=None):
                v = (lambda k: r[n + k]) if c is None else (lambda k: r[n + k].at[c])
                self.wp, self.ra, self.sa, self.rb = v("wp"), v("ra"), v("sa"), v("rb")
                self.sb, self.rc, self.rd = v("sb"), v("rc"), v("rd")
                self.sem = v("sem")
                self.ni = NI if n == "u" else 1

            def put(self, item, t):
                for yy in range(NY):
                    t4 = t[yy * TL * 16 : (yy + 1) * TL * 16].reshape(TL, 2, 8, LANES)
                    for hh in range(2):
                        self.wp[hh, yy, item] = t4[:, hh]

            def a_send(self):
                for k in range(1, NG):
                    gg = (g + k) % NG
                    send(self.wp.at[gg % 2, gg // 2], self.ra.at[k], self.sem.at[0, k], self.sem.at[1, k], gg, d)

            def a_sum_b_send(self):
                for k in range(1, NG):
                    got(self.ra.at[k], self.sem.at[1, k])

                def step(i, carry):
                    t = self.wp[h, y, i]
                    for k in range(1, NG):
                        t = t + self.ra[k, i]
                    t = t.reshape(ZZ, NX, 8, LANES)
                    for xx in range(NX):
                        self.sa[xx, i] = t[:, xx]
                    return carry

                lax.fori_loop(0, self.ni, step, 0)
                for k in range(1, NX):
                    send(self.sa.at[(x + k) % NX], self.rb.at[k], self.sem.at[2, k], self.sem.at[3, k], g, xdev(k))

            def b_sum_z_send(self):
                for k in range(1, NX):
                    got(self.rb.at[k], self.sem.at[3, k])

                def step(i, carry):
                    t = self.sa[x, i]
                    for k in range(1, NX):
                        t = t + self.rb[k, i]
                    for zi in range(ZZ):
                        self.sb[zi, i] = t[zi]
                    return carry

                lax.fori_loop(0, self.ni, step, 0)
                for zi in range(ZZ):
                    zd = y * ZZ + zi
                    k = (zd - z + NZ) % NZ

                    @pl.when(zd != z)
                    def _():
                        rc(
                            self.sb.at[zi], self.rc.at[k], self.sem.at[4, zi], self.sem.at[5, k], g, zd * NX + x
                        ).start()

            def z_sum_c_send(self):
                @pl.when(z // ZZ == y)
                def _():
                    for k in range(1, NZ):
                        got(self.rc.at[k], self.sem.at[5, k])

                    def step(i, carry):
                        t = self.sb[z % ZZ, i]
                        for k in range(1, NZ):
                            t = t + self.rc[k, i]
                        self.rd[h, i] = t
                        return carry

                    lax.fori_loop(0, self.ni, step, 0)
                    for k in range(1, NG):
                        rc(
                            self.rd.at[h], self.rd.at[h], self.sem.at[6, k], self.sem.at[7, h], (g + k) % NG, d
                        ).start()

            def finish(self, outs):
                @pl.when(z // ZZ == y)
                def _():
                    got(self.rd.at[1 - h], self.sem.at[7, 1 - h])
                    for k in range(1, NG):
                        rc(
                            self.rd.at[h], self.rd.at[h], self.sem.at[6, k], self.sem.at[7, h], (g + k) % NG, d
                        ).wait_send()

                @pl.when(z // ZZ != y)
                def _():
                    for hh in range(2):
                        got(self.rd.at[hh], self.sem.at[7, hh])

                for zi in range(ZZ):
                    zd = y * ZZ + zi

                    @pl.when(zd != z)
                    def _():
                        rc(
                            self.sb.at[zi], self.rc.at[0], self.sem.at[4, zi], self.sem.at[5, 0], g, zd * NX + x
                        ).wait_send()

                for i, (k, c) in enumerate(outs):
                    for hh in range(2):
                        r["gw_o"][k, hh * 8 : hh * 8 + 8, c * LANES : (c + 1) * LANES] = self.rd[hh, i] * scale

        red_u = Reduce("u")
        red_m = [Reduce("m", c) for c in range(NCH)]

        def own_grads():
            for c in range(NCH):
                cols = slice(c * LANES, (c + 1) * LANES)
                red_u.put(c, dot(r["agg"][...], r["gp"][:, cols], 0, 0))
                red_u.put(NCH + c, dot(r["nf"][...], r["gp"][:, cols], 0, 0))
            red_u.a_send()

        def final(c):
            partial(c, z)
            if c == 0:
                got(r["hrecv"], r["hr"])
            for dr in range(2):
                got(ring.at[dr, c, HALF], r["rr"].at[dr, c, HALF])
            acc = jnp.zeros((LANES, D), F32)
            for b in range(NB):
                t = summed(z, b) + ring[0, c, HALF, b].astype(F32) + ring[1, c, HALF, b].astype(F32)
                t = t + jnp.where(g > 0, r["hrecv"][c, b].astype(F32), 0.0)
                t = t.astype(BF)
                r["mt"][c, b] = t
                acc = acc + dot(t, r["nf"][b * LANES : (b + 1) * LANES, :], 1, 0)
            red_m[c].put(0, acc.T)
            red_m[c].a_send()

        def nodes_first():
            def step(i, carry):
                rows = pl.ds(pl.multiple_of(i * TR, TR), TR)
                r["gnacc"][rows, :] = r["cot"][rows, :].astype(F32) + dot(r["gp"][rows, :], W[1], 1, 1)
                return carry

            lax.fori_loop(0, R // TR, step, 0)

        def nodes_last():
            def step(b, carry):
                rows = pl.ds(pl.multiple_of(b * LANES, LANES), LANES)
                t = r["gnacc"][rows, :]
                for hh in range(2):
                    per = NCH // 2
                    left = jnp.concatenate([r["mt"][hh * per + c, b].T for c in range(per)], axis=1)
                    t = t + dot(left, M[hh], 1, 1)
                r["gn_o"][rows, :] = t.astype(BF)
                return carry

            lax.fori_loop(0, NB, step, 0)

        def weights_last():
            for k in zorder:
                got(M.at[h, zplane(k)], r["m2r"].at[k])
                send(M.at[h, zplane(k)], M.at[h, zplane(k)], r["m3s"].at[k], r["m3r"].at[k], sib, d)

        xsend(0)
        for k in (1, 3, 2):
            got(r["cin"].at[x], r["cr"].at[k])
        halo(0)
        xforward(0)
        if NCH > 1:
            xsend(1)
        for c in range(1, NCH):
            halo(c)
        send(r["hsend"], r["hrecv"], r["hs"], r["hr"], (g + 1) % NG, d)
        for w in range(NCH + HALF):
            if 0 < w < NCH:
                xforward(w)
                if w + 1 < NCH:
                    xsend(w + 1)
            if w - HALF >= 0:
                final(w - HALF)
            for q in range(HALF - 1, -1, -1):
                c = w - q
                if not 0 <= c < NCH:
                    continue
                if q == 0:
                    xlast(c)
                    ring_step(c, 0, c % 2, False)
                elif q == 1:
                    ring_step(c, 1, c % 2, True)
                    ring_step(c, 1, 1 - c % 2, False)
                else:
                    ring_step(c, q, 0, True)
                    ring_step(c, q, 1, True)
            if w == 0:
                own_grads()
                weights_last()
            if w == 1:
                nodes_first()
            if w == 2:
                red_u.a_sum_b_send()
            if w == 3:
                red_u.b_sum_z_send()
            if w == 4:
                red_u.z_sum_c_send()
            m = w - HALF
            if m >= 1:
                red_m[m - 1].a_sum_b_send()
            if m >= 2:
                red_m[m - 2].b_sum_z_send()
            if m >= 3:
                red_m[m - 3].z_sum_c_send()
        for k in [0] + zorder:
            got(M.at[1 - h, zplane(k)], r["m3r"].at[k])
        nodes_last()
        red_m[NCH - 1].a_sum_b_send()
        if NCH > 1:
            red_m[NCH - 2].b_sum_z_send()
        red_m[NCH - 1].b_sum_z_send()
        for m in range(max(NCH - 3, 0), NCH):
            red_m[m].z_sum_c_send()
        red_u.finish([(1, c) for c in range(NCH)] + [(2, c) for c in range(NCH)])
        for c in range(NCH):
            red_m[c].finish([(0, c)])
        for cp in pending:
            cp.wait_send()

    V = pltpu.VMEM
    S = pltpu.SMEM
    DMA = pltpu.SemaphoreType.DMA
    T2 = (LANES, LANES)
    scratch = [
        ("nf", V((R, D), BF)), ("agg", V((R, D), BF)), ("cot", V((R, D), BF)), ("gp", V((R, D), BF)),
        ("wst", V((2, 16, D), BF)), ("mst", V((2, 16, D // 2), BF)),
        ("W", V((2, D, D), BF)), ("M", V((2, D, D // 2), BF)),
        ("mrecv", V((NX, 8, LANES), jnp.int32)), ("msm", S((NX, 8, LANES), jnp.int32)),
        ("idx", S((NZ, 2 * NSL + NB), jnp.int32)), ("hidx", S((NH + NB,), jnp.int32)),
        ("cin", V((NX, NZ, CAP) + T2, BF)), ("chalo", V((NH,) + T2, BF)),
        ("gown", V((NCH, NB) + T2, BF)),
        ("ebuf", V((NSL + 1,) + T2, F32)), ("hbuf", V((NH + 1,) + T2, F32)),
        ("hsend", V((NCH, NB) + T2, BF)), ("hrecv", V((NCH, NB) + T2, BF)),
        ("ring", V((2, NCH, HALF + 1, NB) + T2, BF)),
        ("mt", V((NCH, NB) + T2, BF)), ("gnacc", V((R, D), F32)),
    ]
    scratch += [("g%d" % c, V((NX * NB + 1,) + T2, BF)) for c in range(NCH)]
    for n, lead, ni in (("u", (), NI), ("m", (NCH,), 1)):
        scratch += [
            (n + "wp", V(lead + (2, NY, ni, TL, 8, LANES), F32)),
            (n + "ra", V(lead + (NG, ni, TL, 8, LANES), F32)),
            (n + "sa", V(lead + (NX, ni, ZZ, 8, LANES), F32)),
            (n + "rb", V(lead + (NX, ni, ZZ, 8, LANES), F32)),
            (n + "sb", V(lead + (ZZ, ni, 8, LANES), F32)),
            (n + "rc", V(lead + (NZ, ni, 8, LANES), F32)),
            (n + "rd", V(lead + (2, ni, 8, LANES), F32)),
            (n + "sem", DMA(lead + (8, max(NG, NZ, NX)))),
        ]
    scratch += [
        ("lsem", DMA((8,))),
        ("w1s", DMA((NX,))), ("w1r", DMA((NX,))), ("m1s", DMA((NX,))), ("m1r", DMA((NX,))),
        ("mts", DMA((NX,))), ("mtr", DMA((NX,))), ("cs", DMA((NX,))), ("cr", DMA((NX,))),
        ("w2s", DMA((NZ,))), ("w2r", DMA((NZ,))), ("w3s", DMA((NZ,))), ("w3r", DMA((NZ,))),
        ("m2s", DMA((NZ,))), ("m2r", DMA((NZ,))), ("m3s", DMA((NZ,))), ("m3r", DMA((NZ,))),
        ("gs", DMA((NCH, 8))), ("gr", DMA((NCH, 8))),
        ("rs", DMA((2, NCH, HALF))), ("rr", DMA((2, NCH, HALF + 1))),
        ("hs", DMA), ("hr", DMA),
    ]
    any_, vm, sm = (pl.BlockSpec(memory_space=m) for m in (pl.ANY, pltpu.VMEM, pltpu.SMEM))
    return pl.pallas_call(
        kernel,
        out_shape=(jax.ShapeDtypeStruct((R, D), BF), jax.ShapeDtypeStruct((3, 16, D), F32)),
        in_specs=[any_] * 6 + [sm, vm, sm, sm, any_, any_],
        out_specs=(vm, vm),
        scratch_shapes=[s for _, s in scratch],
        compiler_params=pltpu.CompilerParams(
            collective_id=0, has_side_effects=True, vmem_limit_bytes=56 * 1024 * 1024
        ),
        cost_estimate=pl.CostEstimate(flops=8 * 10**9, bytes_accessed=10**7, transcendentals=R * D),
    )


def local(
    node_feats,
    aggregate,
    cotangent,
    msg_weight,
    upd_weight,
    self_weight,
    owner_map,
    inner_source,
    inner_target,
    inner_contact,
    send_counts,
    halo_source,
    halo_target,
    halo_contact,
):
    R, D = node_feats.shape
    NG, ND = lax.axis_size("group"), lax.axis_size("dev")
    NZ = ND // NX
    cap = inner_source.shape[0] // ND
    nb = R // LANES

    def per_peer(a):
        return a.reshape(NZ, NX, -1).transpose(1, 0, 2)

    meta = jnp.concatenate([per_peer(inner_source), per_peer(inner_target), per_peer(send_counts)], axis=2)
    meta = jnp.pad(meta, ((0, 0), (0, 8 - NZ), (0, LANES - meta.shape[2])))
    run = make_kernel(NG, ND, R, D, nb, cap, halo_source.shape[0], 1.0 / math.sqrt(R * ND * NG))
    gn, gw = run(
        node_feats, aggregate, cotangent, msg_weight, upd_weight, self_weight, owner_map, meta,
        halo_source, halo_target, inner_contact.reshape(NZ, NX, cap, LANES, LANES), halo_contact,
    )
    return gn, gw[0], gw[1], gw[2]


def solution(mesh):
    both = ("group", "dev")
    in_specs = (
        P(both, None), P(both, None), P(both, None), P("dev", None), P("dev", None), P("dev", None),
        P("group", None), P(both), P(both), P(both, None, None), P(both, None), P(both), P(both),
        P(both, None, None),
    )
    out_specs = (P(both, None), P("dev", None), P("dev", None), P("dev", None))
    return jax.shard_map(local, mesh=mesh, in_specs=in_specs, out_specs=out_specs, check_vma=False)
```

```python
import math
from types import SimpleNamespace

import jax
import jax.numpy as jnp
from jax import lax
from jax.experimental import pallas as pl
from jax.experimental.pallas import tpu as pltpu
from jax.sharding import PartitionSpec as P

BF = jnp.bfloat16
F32 = jnp.float32
NX = 4
LANES = 128
MESH = pl.DeviceIdType.MESH


def dot(a, b, ca, cb):
    return lax.dot_general(a, b, (((ca,), (cb,)), ((), ())), preferred_element_type=F32)


def make_kernel(NG, ND, R, D, NB, CAP, NH, scale):
    NZ = ND // NX
    NY = NG // 2
    ZZ = NZ // NY
    NCH = D // LANES
    NSL = NX * CAP
    HALF = NZ // 2
    TR = min(256, R)
    NI = 2 * NCH
    TL = ZZ * NX
    ZROW = NX * 16
    LY = D // NY
    IP = NI // NY

    def kernel(*refs):
        names = [
            "nf_h", "agg_h", "cot_h", "msg_h", "upd_h", "self_h", "own_s", "isrc_v", "itgt_v", "cnt_v", "hsrc_s", "htgt_s",
            "inner_h", "halo_h", "gn_o", "gw_o",
        ] + [n for n, _ in scratch]
        r = SimpleNamespace(**dict(zip(names, refs)))
        gall = refs[-NCH:]
        g = lax.axis_index("group")
        d = lax.axis_index("dev")
        y, h = g // 2, g % 2
        z, x = d // NX, d % NX
        sib = y * 2 + (1 - h)

        def xdev(k):
            return z * NX + (x + k) % NX

        def zdev(k):
            return ((z + k + NZ) % NZ) * NX + x

        def rc(src, dst, ss, rs, gg, dd):
            return pltpu.make_async_remote_copy(
                src_ref=src, dst_ref=dst, send_sem=ss, recv_sem=rs, device_id=(gg, dd), device_id_type=MESH
            )

        pending = []

        def send(src, dst, ss, rs, gg, dd):
            cp = rc(src, dst, ss, rs, gg, dd)
            cp.start()
            pending.append(cp)

        def got(dst, rs):
            rc(dst, dst, rs, rs, sib, d).wait_recv()

        loads = {}

        def load(name, src, dst, i):
            cp = pltpu.make_async_copy(src, dst, r.lsem.at[i])
            cp.start()
            loads[name] = cp

        HD = D // 2
        load("upd", r.upd_h, r.wst.at[0], 0)
        load("self", r.self_h, r.wst.at[1], 1)
        load("m0", r.msg_h.at[:, pl.ds(0, HD)], r.mst.at[0], 2)
        load("m1", r.msg_h.at[:, pl.ds(HD, HD)], r.mst.at[1], 3)

        load("agg", r.agg_h, r.agg, 8)
        load("nf", r.nf_h, r.nf, 9)
        load("cot", r.cot_h, r.cot, 10)
        load("halo", r.halo_h, r.chalo, 11)
        load("cin", r.inner_h.at[:, x], r.cin.at[x], 4)

        bar = pltpu.get_barrier_semaphore()

        def greet(gg, dd):
            pl.semaphore_signal(bar, inc=1, device_id=(gg, dd), device_id_type=MESH)

        for k in range(1, NX):
            greet(g, xdev(k))
        for k in range(1, NZ):
            greet(g, zdev(k))
        for k in range(1, NG):
            greet((g + k) % NG, d)
        zero = jnp.zeros((LANES, LANES), F32)
        r.ebuf[NSL] = zero
        r.hbuf[NH] = zero
        for c in range(NCH):
            gall[c][NX * NB] = zero.astype(BF)
        for n in ("upd", "self", "m0", "m1"):
            loads[n].wait()
        W, M = r.W, r.M
        row0 = pl.multiple_of(d * 16, 16)
        plane = pl.ds(pl.multiple_of(z * ZROW, 16), ZROW)
        M[h, pl.ds(row0, 16), :] = r.mst[h]
        r.meta[0:1, 0 : ND * CAP] = r.isrc_v[...]
        r.meta[1:2, 0 : ND * CAP] = r.itgt_v[...]
        r.meta[2:3, 0:ND] = r.cnt_v[...]
        r.mrecv[x] = r.meta[...]
        pl.semaphore_wait(bar, NX - 1 + NZ - 1 + NG - 1)

        myrow = pl.ds(row0, 16)

        def lanes(j):
            return pl.ds(pl.multiple_of(((y - j + NY) % NY) * LY, LANES), LY)

        def wpart(core, rows, j):
            return W.at[core, rows, lanes(j)]

        for k in (1, 3, 2):
            send(r.wst.at[h, :, lanes(0)], wpart(h, myrow, 0), r.w1s.at[k], r.w1r.at[k], g, xdev(k))
        load("w", r.wst.at[h, :, lanes(0)], wpart(h, myrow, 0), 6)
        for k in (1, 3, 2):
            send(r.mst.at[h], M.at[h, myrow], r.m1s.at[k], r.m1r.at[k], g, xdev(k))
            send(r.meta, r.mrecv.at[x], r.mts.at[k], r.mtr.at[k], g, xdev(k))

        def csend(dd):
            for off in sorted({dd % NZ, (NZ - dd) % NZ}):
                zt = (z + off) % NZ
                for k in (1, 3, 2):
                    send(
                        r.inner_h.at[zt, (x + k) % NX], r.cin.at[x, zt], r.cs.at[off, k], r.cr.at[off, k],
                        g, xdev(k),
                    )

        have = set()

        def cgot(off):
            if off in have:
                return
            have.add(off)
            zt = (z + off) % NZ
            for k in (1, 3, 2):
                got(r.cin.at[(x - k + NX) % NX, zt], r.cr.at[off, k])

        for dd in range(HALF, 1, -1):
            csend(dd)
        for k in (1, 3, 2):
            got(wpart(h, myrow, 0), r.w1r.at[k])
        loads["w"].wait()
        zorder = sorted(range(1, NZ), key=lambda k: min(k, NZ - k))

        def zplane(k):
            return pl.ds(pl.multiple_of(((z - k + NZ) % NZ) * ZROW, 16), ZROW)

        def hand_on(k):
            part = wpart(h, zplane(k), 0)
            for j in range(1, NY):
                send(part, part, r.wys.at[j, k], r.wyr.at[j, k], ((y + j) % NY) * 2 + h, d)
            send(part, part, r.w3s.at[k], r.w3r.at[k], sib, d)

        for k in zorder[::-1]:
            part = wpart(h, plane, 0)
            send(part, part, r.w2s.at[k], r.w2r.at[k], g, zdev(k))
        hand_on(0)
        for k in (1, 3, 2):
            got(M.at[h, myrow], r.m1r.at[k])
            got(r.mrecv.at[x], r.mtr.at[k])
        meta_in = pltpu.make_async_copy(r.mrecv, r.msm, r.lsem.at[5])
        meta_in.start()
        for k in zorder:
            got(wpart(h, zplane(k), 0), r.w2r.at[k])
            hand_on(k)
        for k in range(1, NZ):
            send(M.at[h, plane], M.at[h, plane], r.m2s.at[k], r.m2r.at[k], g, zdev(k))
        send(M.at[h, plane], M.at[h, plane], r.m3s.at[0], r.m3r.at[0], sib, d)

        for j in range(1, NY):
            for k in [0] + zorder:
                got(wpart(h, zplane(k), j), r.wyr.at[j, k])
            part = wpart(h, pl.ds(0, D), j)
            send(part, part, r.wbs.at[j], r.wbr.at[j], sib, d)
        for k in [0] + zorder:
            got(wpart(1 - h, zplane(k), 0), r.w3r.at[k])
        for j in range(1, NY):
            got(wpart(1 - h, pl.ds(0, D), j), r.wbr.at[j])
        for n in ("agg", "nf", "cot", "halo", "cin"):
            loads[n].wait()

        def hstep(s, last):
            src = r.hsrc_s[s]
            prev = jnp.int32(NH)
            for b in range(NB):
                prev = jnp.where(src == b, last[b], prev)
            r.hidx[s] = prev
            return tuple(jnp.where(src == b, s, last[b]) for b in range(NB))


        def istep(zt, carry):
            dst = []
            for s in range(NSL):
                xs, cc = s // CAP, s % CAP
                peer = zt * NX + x
                dst.append(lax.rem(r.own_s[0, r.msm[xs, 0, peer * CAP + cc]], NB))
                r.idx[zt, s] = jnp.where(
                    cc < r.msm[xs, 2, peer], xs * NB + r.msm[xs, 1, peer * CAP + cc], NX * NB
                )
            for s in range(NSL):
                p = jnp.int32(NSL)
                for j in range(s):
                    p = jnp.where(dst[j] == dst[s], j, p)
                r.idx[zt, NSL + s] = p
            for b in range(NB):
                p = jnp.int32(NSL)
                for j in range(NSL):
                    p = jnp.where(dst[j] == b, j, p)
                r.idx[zt, 2 * NSL + b] = p
            return carry

        def indices():
            last = lax.fori_loop(0, NH, hstep, (jnp.int32(NH),) * NB)
            for b in range(NB):
                r.hidx[NH + b] = last[b]
            meta_in.wait()
            lax.fori_loop(0, NZ, istep, 0)

        NT = R // TR
        TB = TR // LANES

        def tile_send(i, k):
            return rc(
                r.gown.at[0, pl.ds(i * TB, TB)], gall[0].at[pl.ds(x * NB + i * TB, TB)],
                r.g0s.at[i, k], r.g0r.at[i, k], g, xdev(k),
            )

        def tile_got(i, k):
            got(gall[0].at[pl.ds((x - k + NX) % NX * NB + i * TB, TB)], r.g0r.at[i, k])

        def pstep(i, carry):
            rows = pl.ds(pl.multiple_of(i * TR, TR), TR)
            pre = dot(r.agg[rows, :], W[0], 1, 0) + dot(r.nf[rows, :], W[1], 1, 0)
            sg = jax.nn.sigmoid(pre)
            gp = (r.cot[rows, :].astype(F32) * sg * (1.0 + pre * (1.0 - sg))).astype(BF)
            r.gp[rows, :] = gp
            gt = dot(W[0], gp, 1, 1).astype(BF)
            for t in range(TR // LANES):
                for c in range(NCH):
                    tile = gt[c * LANES : (c + 1) * LANES, t * LANES : (t + 1) * LANES]
                    r.gown[c, i * (TR // LANES) + t] = tile
                    gall[c][x * NB + i * (TR // LANES) + t] = tile
            for k in (1, 3):
                tile_send(i, k).start()
            return carry

        lax.fori_loop(0, NT, pstep, 0)

        NHB = NB // 2

        def xsend(c):
            for k in (1, 3):
                send(
                    r.gown.at[c], gall[c].at[pl.ds(x * NB, NB)], r.gs.at[c, k], r.gr.at[c, k], g, xdev(k)
                )

        def xforward(c):
            for k, off in ((1, 0), (3, NHB)):
                xs = (x - k + NX) % NX
                if c == 0:
                    for i in range(NT // 2):
                        tile_got(i + off // TB, k)
                else:
                    got(gall[c].at[pl.ds(xs * NB, NB)], r.gr.at[c, k])
                part = gall[c].at[pl.ds(xs * NB + off, NHB)]
                send(part, part, r.gs.at[c, 4 + k], r.gr.at[c, 4 + k], g, xdev(k))

        def xlast(c):
            xs = (x + 2) % NX
            if c == 0:
                for k, off in ((1, NHB), (3, 0)):
                    for i in range(NT // 2):
                        tile_got(i + off // TB, k)
            for k, off in ((1, 0), (3, NHB)):
                got(gall[c].at[pl.ds(xs * NB + off, NHB)], r.gr.at[c, 4 + k])

        def halo(c):
            def step(i, carry):
                for j in range(8):
                    s = i * 8 + j
                    r.hbuf[s] = dot(r.gown[c, r.htgt_s[s]], r.chalo[s], 1, 0)
                for j in range(8):
                    s = i * 8 + j
                    r.hbuf[s] = r.hbuf[s] + r.hbuf[r.hidx[s]]
                return carry

            lax.fori_loop(0, NH // 8, step, 0)
            for b in range(NB):
                r.hsend[c, b] = r.hbuf[r.hidx[NH + b]].astype(BF)
            send(r.hsend.at[c], r.hrecv.at[c], r.hs.at[c], r.hr.at[c], (g + 1) % NG, d)

        ring = r.ring

        def partial(c, zt):
            for s in range(NSL):
                r.ebuf[s] = dot(gall[c][r.idx[zt, s]], r.cin[s // CAP, zt, s % CAP], 1, 0)
            for s in range(1, NSL):
                r.ebuf[s] = r.ebuf[s] + r.ebuf[r.idx[zt, NSL + s]]

        def summed(zt, b):
            return r.ebuf[r.idx[zt, 2 * NSL + b]]

        def ring_step(c, q, dr, has_recv):
            dd = HALF - q
            sgn = 1 - 2 * dr
            zt = (z + sgn * dd + NZ) % NZ
            cgot((sgn * dd) % NZ)
            partial(c, zt)
            slot = ring.at[dr, c, q]
            if has_recv:
                got(slot, r.rr.at[dr, c, q])
                for b in range(NB):
                    ring[dr, c, q, b] = (summed(zt, b) + ring[dr, c, q, b].astype(F32)).astype(BF)
            else:
                for b in range(NB):
                    ring[dr, c, q, b] = summed(zt, b).astype(BF)
            nz = ((z + sgn + NZ) % NZ) * NX + x
            cp = rc(slot, ring.at[dr, c, q + 1], r.rs.at[dr, c, q], r.rr.at[dr, c, q + 1], g, nz)
            cp.start()
            pending.append(cp)

        class Reduce:
            def __init__(self, c):
                self.wp, self.ra, self.sa, self.rb = r.mwp.at[c], r.mra.at[c], r.msa.at[c], r.mrb.at[c]
                self.sb, self.rc, self.rd = r.msb.at[c], r.mrc.at[c], r.mrd.at[c]
                self.sem = r.msem.at[c]
                self.ni = 1

            def put(self, item, t):
                for yy in range(NY):
                    t4 = t[yy * TL * 16 : (yy + 1) * TL * 16].reshape(TL, 2, 8, LANES)
                    for hh in range(2):
                        self.wp[hh, yy, item] = t4[:, hh]

            def a_send(self):
                for k in range(1, NG):
                    gg = (g + k) % NG
                    send(self.wp.at[gg % 2, gg // 2], self.ra.at[k], self.sem.at[0, k], self.sem.at[1, k], gg, d)

            def a_sum_b_send(self):
                for k in range(1, NG):
                    got(self.ra.at[k], self.sem.at[1, k])

                def step(i, carry):
                    t = self.wp[h, y, i]
                    for k in range(1, NG):
                        t = t + self.ra[k, i]
                    t = t.reshape(ZZ, NX, 8, LANES)
                    for xx in range(NX):
                        self.sa[xx, i] = t[:, xx]
                    return carry

                lax.fori_loop(0, self.ni, step, 0)
                for k in range(1, NX):
                    send(self.sa.at[(x + k) % NX], self.rb.at[k], self.sem.at[2, k], self.sem.at[3, k], g, xdev(k))

            def b_sum_z_send(self):
                for k in range(1, NX):
                    got(self.rb.at[k], self.sem.at[3, k])

                def step(i, carry):
                    t = self.sa[x, i]
                    for k in range(1, NX):
                        t = t + self.rb[k, i]
                    for zi in range(ZZ):
                        self.sb[zi, i] = t[zi]
                    return carry

                lax.fori_loop(0, self.ni, step, 0)
                for zi in range(ZZ):
                    zd = y * ZZ + zi
                    k = (zd - z + NZ) % NZ

                    @pl.when(zd != z)
                    def _():
                        rc(
                            self.sb.at[zi], self.rc.at[k], self.sem.at[4, zi], self.sem.at[5, k], g, zd * NX + x
                        ).start()

            def z_sum_c_send(self):
                @pl.when(z // ZZ == y)
                def _():
                    for k in range(1, NZ):
                        got(self.rc.at[k], self.sem.at[5, k])

                    def step(i, carry):
                        t = self.sb[z % ZZ, i]
                        for k in range(1, NZ):
                            t = t + self.rc[k, i]
                        self.rd[h, i] = t
                        return carry

                    lax.fori_loop(0, self.ni, step, 0)
                    for k in range(1, NG):
                        rc(
                            self.rd.at[h], self.rd.at[h], self.sem.at[6, k], self.sem.at[7, h], (g + k) % NG, d
                        ).start()

            def finish(self, outs):
                @pl.when(z // ZZ == y)
                def _():
                    got(self.rd.at[1 - h], self.sem.at[7, 1 - h])
                    for k in range(1, NG):
                        rc(
                            self.rd.at[h], self.rd.at[h], self.sem.at[6, k], self.sem.at[7, h], (g + k) % NG, d
                        ).wait_send()

                @pl.when(z // ZZ != y)
                def _():
                    for hh in range(2):
                        got(self.rd.at[hh], self.sem.at[7, hh])

                for zi in range(ZZ):
                    zd = y * ZZ + zi

                    @pl.when(zd != z)
                    def _():
                        rc(
                            self.sb.at[zi], self.rc.at[0], self.sem.at[4, zi], self.sem.at[5, 0], g, zd * NX + x
                        ).wait_send()

                for i, (k, c) in enumerate(outs):
                    for hh in range(2):
                        r.gw_o[k, hh * 8 : hh * 8 + 8, c * LANES : (c + 1) * LANES] = self.rd[hh, i] * scale

        class ReduceItems:
            def a_send(self):
                for k in range(1, NG):
                    gg = (g + k) % NG
                    part = r.uwp.at[gg % 2, pl.ds((gg // 2) * IP, IP)]
                    send(part, r.ura.at[k], r.usem.at[0, k], r.usem.at[1, k], gg, d)

            def put(self, item, t):
                t4 = t.reshape(ND, 2, 8, LANES)
                for hh in range(2):
                    r.uwp[hh, item] = t4[:, hh]

            def a_sum_b_send(self):
                for k in range(1, NG):
                    got(r.ura.at[k], r.usem.at[1, k])

                def step(i, carry):
                    t = r.uwp[h, y * IP + i]
                    for k in range(1, NG):
                        t = t + r.ura[k, i]
                    t = t.reshape(NZ, NX, 8, LANES)
                    for xx in range(NX):
                        r.usa[xx, i] = t[:, xx]
                    return carry

                lax.fori_loop(0, IP, step, 0)
                for k in range(1, NX):
                    send(
                        r.usa.at[(x + k) % NX], r.urb.at[k], r.usem.at[2, k], r.usem.at[3, k], g, xdev(k)
                    )

            def b_sum_z_send(self):
                for k in range(1, NX):
                    got(r.urb.at[k], r.usem.at[3, k])
                for i in range(IP):
                    t = r.usa[x, i]
                    for k in range(1, NX):
                        t = t + r.urb[k, i]
                    for zd in range(NZ):
                        r.usb[zd, i] = t[zd]
                for k in range(1, NZ):
                    send(
                        r.usb.at[(z + k) % NZ], r.urc.at[k], r.usem.at[4, k], r.usem.at[5, k], g, zdev(k)
                    )

            def z_sum_c_send(self):
                for k in range(1, NZ):
                    got(r.urc.at[k], r.usem.at[5, k])
                for i in range(IP):
                    t = r.usb[z, i]
                    for k in range(1, NZ):
                        t = t + r.urc[k, i]
                    r.urd[h, y, i] = t
                part = r.urd.at[h, y]
                for k in range(1, NG):
                    send(part, part, r.usem.at[6, k], r.usem.at[7, k], (g + k) % NG, d)

            def finish(self, outs):
                for k in range(1, NG):
                    gg = (g - k + NG) % NG
                    got(r.urd.at[gg % 2, gg // 2], r.usem.at[7, k])
                for i, (k, c) in enumerate(outs):
                    for hh in range(2):
                        r.gw_o[k, hh * 8 : hh * 8 + 8, c * LANES : (c + 1) * LANES] = (
                            r.urd[hh, i // IP, i % IP] * scale
                        )

        red_u = ReduceItems()
        red_m = [Reduce(c) for c in range(NCH)]

        def own_grads():
            for c in range(NCH):
                cols = slice(c * LANES, (c + 1) * LANES)
                red_u.put(c, dot(r.agg[...], r.gp[:, cols], 0, 0))
                red_u.put(NCH + c, dot(r.nf[...], r.gp[:, cols], 0, 0))
            red_u.a_send()

        def final(c):
            cgot(0)
            partial(c, z)
            got(r.hrecv.at[c], r.hr.at[c])
            for dr in range(2):
                got(ring.at[dr, c, HALF], r.rr.at[dr, c, HALF])
            acc = jnp.zeros((LANES, D), F32)
            for b in range(NB):
                t = summed(z, b) + ring[0, c, HALF, b].astype(F32) + ring[1, c, HALF, b].astype(F32)
                t = t + jnp.where(g > 0, r.hrecv[c, b].astype(F32), 0.0)
                t = t.astype(BF)
                r.mt[c, b] = t
                acc = acc + dot(t, r.nf[b * LANES : (b + 1) * LANES, :], 1, 0)
            red_m[c].put(0, acc.T)
            red_m[c].a_send()

        def nodes_first():
            def step(i, carry):
                rows = pl.ds(pl.multiple_of(i * TR, TR), TR)
                r.gnacc[rows, :] = r.cot[rows, :].astype(F32) + dot(r.gp[rows, :], W[1], 1, 1)
                return carry

            lax.fori_loop(0, R // TR, step, 0)

        def nodes_last():
            def step(b, carry):
                rows = pl.ds(pl.multiple_of(b * LANES, LANES), LANES)
                t = r.gnacc[rows, :]
                for hh in range(2):
                    per = NCH // 2
                    left = jnp.concatenate([r.mt[hh * per + c, b].T for c in range(per)], axis=1)
                    t = t + dot(left, M[hh], 1, 1)
                r.cot[rows, :] = t.astype(BF)
                return carry

            lax.fori_loop(0, NB, step, 0)
            load("out", r.cot, r.gn_o, 7)

        def weights_last():
            for k in zorder:
                got(M.at[h, zplane(k)], r.m2r.at[k])
                send(M.at[h, zplane(k)], M.at[h, zplane(k)], r.m3s.at[k], r.m3r.at[k], sib, d)

        indices()
        halo(0)
        xforward(0)
        if NCH > 1:
            xsend(1)
        for w in range(NCH + HALF):
            if 0 < w < NCH:
                xforward(w)
                if w == 1:
                    csend(1)
                if w + 1 < NCH:
                    xsend(w + 1)
            if w == 2:
                csend(0)
            chunks = [c for c in range(NCH) if 0 <= w - c < HALF]
            for c in chunks if w < 3 else chunks[::-1]:
                p = w - c
                if p == 0:
                    xlast(c)
                ring_step(c, p, c % 2, p > 0)
                if p + 1 < HALF:
                    ring_step(c, p + 1, 1 - c % 2, p > 0)
            if w - HALF >= 0:
                final(w - HALF)
            if w == 0:
                weights_last()
            if w + 1 < NCH:
                halo(w + 1)
            if w == 1:
                own_grads()
            if w == 3:
                red_u.a_sum_b_send()
            if w == 4:
                red_u.b_sum_z_send()
                nodes_first()
            if w == 5:
                red_u.z_sum_c_send()
            m = w - HALF
            if m >= 1:
                red_m[m - 1].a_sum_b_send()
            if m >= 2:
                red_m[m - 2].b_sum_z_send()
            if m >= 3:
                red_m[m - 3].z_sum_c_send()
        for k in [0] + zorder:
            got(M.at[1 - h, zplane(k)], r.m3r.at[k])
        nodes_last()
        red_m[NCH - 1].a_sum_b_send()
        if NCH > 1:
            red_m[NCH - 2].b_sum_z_send()
        red_m[NCH - 1].b_sum_z_send()
        for m in range(max(NCH - 3, 0), NCH):
            red_m[m].z_sum_c_send()
        red_u.finish([(1, c) for c in range(NCH)] + [(2, c) for c in range(NCH)])
        for c in range(NCH):
            red_m[c].finish([(0, c)])
        for i in range(NT):
            for k in (1, 3):
                tile_send(i, k).wait_send()
        for cp in pending:
            cp.wait_send()
        loads["out"].wait()

    V = pltpu.VMEM
    S = pltpu.SMEM
    DMA = pltpu.SemaphoreType.DMA
    T2 = (LANES, LANES)
    scratch = [
        ("nf", V((R, D), BF)), ("agg", V((R, D), BF)), ("cot", V((R, D), BF)), ("gp", V((R, D), BF)),
        ("wst", V((2, 16, D), BF)), ("mst", V((2, 16, D // 2), BF)),
        ("W", V((2, D, D), BF)), ("M", V((2, D, D // 2), BF)),
        ("meta", V((8, LANES), jnp.int32)), ("mrecv", V((NX, 8, LANES), jnp.int32)), ("msm", S((NX, 8, LANES), jnp.int32)),
        ("idx", S((NZ, 2 * NSL + NB), jnp.int32)), ("hidx", S((NH + NB,), jnp.int32)),
        ("cin", V((NX, NZ, CAP) + T2, BF)), ("chalo", V((NH,) + T2, BF)),
        ("gown", V((NCH, NB) + T2, BF)),
        ("ebuf", V((NSL + 1,) + T2, F32)), ("hbuf", V((NH + 1,) + T2, F32)),
        ("hsend", V((NCH, NB) + T2, BF)), ("hrecv", V((NCH, NB) + T2, BF)),
        ("ring", V((2, NCH, HALF + 1, NB) + T2, BF)),
        ("mt", V((NCH, NB) + T2, BF)), ("gnacc", V((R, D), F32)),
    ]
    scratch += [
        ("uwp", V((2, NI, ND, 8, LANES), F32)), ("ura", V((NG, IP, ND, 8, LANES), F32)),
        ("usa", V((NX, IP, NZ, 8, LANES), F32)), ("urb", V((NX, IP, NZ, 8, LANES), F32)),
        ("usb", V((NZ, IP, 8, LANES), F32)), ("urc", V((NZ, IP, 8, LANES), F32)),
        ("urd", V((2, NY, IP, 8, LANES), F32)), ("usem", DMA((8, max(NG, NZ, NX)))),
    ]
    for n, lead, ni in (("m", (NCH,), 1),):
        scratch += [
            (n + "wp", V(lead + (2, NY, ni, TL, 8, LANES), F32)),
            (n + "ra", V(lead + (NG, ni, TL, 8, LANES), F32)),
            (n + "sa", V(lead + (NX, ni, ZZ, 8, LANES), F32)),
            (n + "rb", V(lead + (NX, ni, ZZ, 8, LANES), F32)),
            (n + "sb", V(lead + (ZZ, ni, 8, LANES), F32)),
            (n + "rc", V(lead + (NZ, ni, 8, LANES), F32)),
            (n + "rd", V(lead + (2, ni, 8, LANES), F32)),
            (n + "sem", DMA(lead + (8, max(NG, NZ, NX)))),
        ]
    scratch += [
        ("lsem", DMA((12,))),
        ("w1s", DMA((NX,))), ("w1r", DMA((NX,))), ("m1s", DMA((NX,))), ("m1r", DMA((NX,))),
        ("mts", DMA((NX,))), ("mtr", DMA((NX,))), ("cs", DMA((NZ, NX))), ("cr", DMA((NZ, NX))),
        ("w2s", DMA((NZ,))), ("w2r", DMA((NZ,))), ("w3s", DMA((NZ,))), ("w3r", DMA((NZ,))),
        ("m2s", DMA((NZ,))), ("m2r", DMA((NZ,))), ("m3s", DMA((NZ,))), ("m3r", DMA((NZ,))),
        ("g0s", DMA((R // TR, NX))), ("g0r", DMA((R // TR, NX))), ("gs", DMA((NCH, 8))), ("gr", DMA((NCH, 8))),
        ("rs", DMA((2, NCH, HALF))), ("rr", DMA((2, NCH, HALF + 1))),
        ("hs", DMA((NCH,))), ("hr", DMA((NCH,))),
        ("wys", DMA((NY, NZ))), ("wyr", DMA((NY, NZ))), ("wbs", DMA((NY,))), ("wbr", DMA((NY,))),
    ]
    scratch += [("g%d" % c, V((NX * NB + 1,) + T2, BF)) for c in range(NCH)]
    any_, vm, sm = (pl.BlockSpec(memory_space=m) for m in (pl.ANY, pltpu.VMEM, pltpu.SMEM))
    return pl.pallas_call(
        kernel,
        out_shape=(jax.ShapeDtypeStruct((R, D), BF), jax.ShapeDtypeStruct((3, 16, D), F32)),
        in_specs=[any_] * 6 + [sm, vm, vm, vm, sm, sm, any_, any_],
        out_specs=(any_, vm),
        scratch_shapes=[s for _, s in scratch],
        compiler_params=pltpu.CompilerParams(
            collective_id=0, has_side_effects=True, vmem_limit_bytes=56 * 1024 * 1024
        ),
        cost_estimate=pl.CostEstimate(flops=8 * 10**9, bytes_accessed=10**7, transcendentals=R * D),
    )


def local(
    node_feats,
    aggregate,
    cotangent,
    msg_weight,
    upd_weight,
    self_weight,
    owner_map,
    inner_source,
    inner_target,
    inner_contact,
    send_counts,
    halo_source,
    halo_target,
    halo_contact,
):
    R, D = node_feats.shape
    NG, ND = lax.axis_size("group"), lax.axis_size("dev")
    NZ = ND // NX
    cap = inner_source.shape[0] // ND
    nb = R // LANES

    run = make_kernel(NG, ND, R, D, nb, cap, halo_source.shape[0], 1.0 / math.sqrt(R * ND * NG))
    gn, gw = run(
        node_feats, aggregate, cotangent, msg_weight, upd_weight, self_weight, owner_map,
        inner_source.reshape(1, -1), inner_target.reshape(1, -1), send_counts, halo_source, halo_target, inner_contact.reshape(NZ, NX, cap, LANES, LANES), halo_contact,
    )
    return gn, gw[0], gw[1], gw[2]


def solution(mesh):
    both = ("group", "dev")
    in_specs = (
        P(both, None), P(both, None), P(both, None), P("dev", None), P("dev", None), P("dev", None),
        P("group", None), P(both), P(both), P(both, None, None), P(both, None), P(both), P(both),
        P(both, None, None),
    )
    out_specs = (P(both, None), P("dev", None), P("dev", None), P("dev", None))
    return jax.shard_map(local, mesh=mesh, in_specs=in_specs, out_specs=out_specs, check_vma=False)
```

```python
import math
from types import SimpleNamespace

import jax
import jax.numpy as jnp
from jax import lax
from jax.experimental import pallas as pl
from jax.experimental.pallas import tpu as pltpu
from jax.sharding import PartitionSpec as P

BF = jnp.bfloat16
F32 = jnp.float32
NX = 4
LANES = 128
MESH = pl.DeviceIdType.MESH


def dot(a, b, ca, cb):
    return lax.dot_general(a, b, (((ca,), (cb,)), ((), ())), preferred_element_type=F32)


def make_kernel(NG, ND, R, D, NB, CAP, NH, scale):
    NZ = ND // NX
    NY = NG // 2
    ZZ = NZ // NY
    NCH = D // LANES
    NSL = NX * CAP
    HALF = NZ // 2
    TR = min(256, R)
    NI = 2 * NCH
    TL = ZZ * NX
    ZROW = NX * 16
    LY = D // NY
    IP = NI // NY

    def kernel(*refs):
        names = [
            "nf_h", "agg_h", "cot_h", "msg_h", "upd_h", "self_h", "own_h", "isrc_h", "itgt_h", "cnt_h", "hsrc_h", "htgt_h",
            "inner_h", "halo_h", "gn_o", "gw_o",
        ] + [n for n, _ in scratch]
        r = SimpleNamespace(**dict(zip(names, refs)))
        gall = refs[-NCH:]
        g = lax.axis_index("group")
        d = lax.axis_index("dev")
        y, h = g // 2, g % 2
        z, x = d // NX, d % NX
        sib = y * 2 + (1 - h)

        def xdev(k):
            return z * NX + (x + k) % NX

        def zdev(k):
            return ((z + k + NZ) % NZ) * NX + x

        def rc(src, dst, ss, rs, gg, dd):
            return pltpu.make_async_remote_copy(
                src_ref=src, dst_ref=dst, send_sem=ss, recv_sem=rs, device_id=(gg, dd), device_id_type=MESH
            )

        pending = []

        def send(src, dst, ss, rs, gg, dd):
            cp = rc(src, dst, ss, rs, gg, dd)
            cp.start()
            pending.append(cp)

        def got(dst, rs):
            rc(dst, dst, rs, rs, sib, d).wait_recv()

        bar = pltpu.get_barrier_semaphore()

        def greet(gg, dd):
            pl.semaphore_signal(bar, inc=1, device_id=(gg, dd), device_id_type=MESH)

        for k in range(1, NX):
            greet(g, xdev(k))
        for k in range(1, NZ):
            greet(g, zdev(k))
        for k in range(1, NG):
            greet((g + k) % NG, d)

        loads = {}

        def load(name, src, dst, i):
            cp = pltpu.make_async_copy(src, dst, r.lsem.at[i])
            cp.start()
            loads[name] = cp

        HD = D // 2
        load("upd", r.upd_h, r.wst.at[0], 0)
        load("self", r.self_h, r.wst.at[1], 1)
        load("isrc", r.isrc_h, r.isrc_v, 12)
        load("itgt", r.itgt_h, r.itgt_v, 13)
        load("cnt", r.cnt_h, r.cnt_v, 14)
        load("m0", r.msg_h.at[:, pl.ds(0, HD)], r.mst.at[0], 2)
        load("m1", r.msg_h.at[:, pl.ds(HD, HD)], r.mst.at[1], 3)

        load("own", r.own_h, r.own_s, 15)
        load("hsrc", r.hsrc_h, r.hsrc_s, 16)
        load("htgt", r.htgt_h, r.htgt_s, 17)
        load("agg", r.agg_h, r.agg, 8)
        load("nf", r.nf_h, r.nf, 9)
        load("cot", r.cot_h, r.cot, 10)
        load("halo", r.halo_h, r.chalo, 11)
        load("cin", r.inner_h.at[:, x], r.cin.at[x], 4)

        zero = jnp.zeros((LANES, LANES), F32)
        r.ebuf[NSL] = zero
        r.hbuf[NH] = zero
        for c in range(NCH):
            gall[c][NX * NB] = zero.astype(BF)
        for n in ("upd", "self", "m0", "m1", "isrc", "itgt", "cnt"):
            loads[n].wait()
        W, M = r.W, r.M
        row0 = pl.multiple_of(d * 16, 16)
        plane = pl.ds(pl.multiple_of(z * ZROW, 16), ZROW)
        M[h, pl.ds(row0, 16), :] = r.mst[h]
        r.meta[0:1, 0 : ND * CAP] = r.isrc_v[...]
        r.meta[1:2, 0 : ND * CAP] = r.itgt_v[...]
        r.meta[2:3, 0:ND] = r.cnt_v[...]
        r.mrecv[x] = r.meta[...]
        pl.semaphore_wait(bar, NX - 1 + NZ - 1 + NG - 1)

        myrow = pl.ds(row0, 16)

        def lanes(j):
            return pl.ds(pl.multiple_of(((y - j + NY) % NY) * LY, LANES), LY)

        def wpart(core, rows, j):
            return W.at[core, rows, lanes(j)]

        for k in (1, 3, 2):
            send(r.wst.at[h, :, lanes(0)], wpart(h, myrow, 0), r.w1s.at[k], r.w1r.at[k], g, xdev(k))
        load("w", r.wst.at[h, :, lanes(0)], wpart(h, myrow, 0), 6)
        for k in (1, 3, 2):
            send(r.mst.at[h], M.at[h, myrow], r.m1s.at[k], r.m1r.at[k], g, xdev(k))
            send(r.meta, r.mrecv.at[x], r.mts.at[k], r.mtr.at[k], g, xdev(k))

        def csend(dd):
            for off in sorted({dd % NZ, (NZ - dd) % NZ}):
                zt = (z + off) % NZ
                for k in (1, 3, 2):
                    send(
                        r.inner_h.at[zt, (x + k) % NX], r.cin.at[x, zt], r.cs.at[off, k], r.cr.at[off, k],
                        g, xdev(k),
                    )

        have = set()

        def cgot(off):
            if off in have:
                return
            have.add(off)
            zt = (z + off) % NZ
            for k in (1, 3, 2):
                got(r.cin.at[(x - k + NX) % NX, zt], r.cr.at[off, k])

        for k in (1, 3, 2):
            got(wpart(h, myrow, 0), r.w1r.at[k])
        loads["w"].wait()
        zorder = sorted(range(1, NZ), key=lambda k: min(k, NZ - k))

        def zplane(k):
            return pl.ds(pl.multiple_of(((z - k + NZ) % NZ) * ZROW, 16), ZROW)

        def hand_on(k):
            part = wpart(h, zplane(k), 0)
            for j in range(1, NY):
                send(part, part, r.wys.at[j, k], r.wyr.at[j, k], ((y + j) % NY) * 2 + h, d)
            send(part, part, r.w3s.at[k], r.w3r.at[k], sib, d)

        for k in zorder[::-1]:
            part = wpart(h, plane, 0)
            send(part, part, r.w2s.at[k], r.w2r.at[k], g, zdev(k))
        hand_on(0)
        for dd in range(HALF, 1, -1):
            csend(dd)
        for k in (1, 3, 2):
            got(M.at[h, myrow], r.m1r.at[k])
            got(r.mrecv.at[x], r.mtr.at[k])
        meta_in = pltpu.make_async_copy(r.mrecv, r.msm, r.lsem.at[5])
        meta_in.start()
        def hstep(s, last):
            src = r.hsrc_s[s]
            prev = jnp.int32(NH)
            for b in range(NB):
                prev = jnp.where(src == b, last[b], prev)
            r.hidx[s] = prev
            return tuple(jnp.where(src == b, s, last[b]) for b in range(NB))


        for n in ("own", "hsrc", "htgt"):
            loads[n].wait()
        last = lax.fori_loop(0, NH, hstep, (jnp.int32(NH),) * NB)
        for b in range(NB):
            r.hidx[NH + b] = last[b]

        for k in zorder:
            got(wpart(h, zplane(k), 0), r.w2r.at[k])
            hand_on(k)
        for k in range(1, NZ):
            send(M.at[h, plane], M.at[h, plane], r.m2s.at[k], r.m2r.at[k], g, zdev(k))
        send(M.at[h, plane], M.at[h, plane], r.m3s.at[0], r.m3r.at[0], sib, d)

        def istep(zt, carry):
            dst = []
            for s in range(NSL):
                xs, cc = s // CAP, s % CAP
                peer = zt * NX + x
                dst.append(lax.rem(r.own_s[0, r.msm[xs, 0, peer * CAP + cc]], NB))
                r.idx[zt, s] = jnp.where(
                    cc < r.msm[xs, 2, peer], xs * NB + r.msm[xs, 1, peer * CAP + cc], NX * NB
                )
            for s in range(NSL):
                p = jnp.int32(NSL)
                for j in range(s):
                    p = jnp.where(dst[j] == dst[s], j, p)
                r.idx[zt, NSL + s] = p
            for b in range(NB):
                p = jnp.int32(NSL)
                for j in range(NSL):
                    p = jnp.where(dst[j] == b, j, p)
                r.idx[zt, 2 * NSL + b] = p
            return carry

        meta_in.wait()
        lax.fori_loop(0, NZ, istep, 0)

        for j in range(1, NY):
            for k in [0] + zorder:
                got(wpart(h, zplane(k), j), r.wyr.at[j, k])
            part = wpart(h, pl.ds(0, D), j)
            send(part, part, r.wbs.at[j], r.wbr.at[j], sib, d)
        for k in [0] + zorder:
            got(wpart(1 - h, zplane(k), 0), r.w3r.at[k])
        for j in range(1, NY):
            got(wpart(1 - h, pl.ds(0, D), j), r.wbr.at[j])
        for n in ("agg", "nf", "cot", "halo", "cin"):
            loads[n].wait()

        NT = R // TR
        TB = TR // LANES

        def tile_send(i, k):
            return rc(
                r.gown.at[0, pl.ds(i * TB, TB)], gall[0].at[pl.ds(x * NB + i * TB, TB)],
                r.g0s.at[i, k], r.g0r.at[i, k], g, xdev(k),
            )

        def tile_got(i, k):
            got(gall[0].at[pl.ds((x - k + NX) % NX * NB + i * TB, TB)], r.g0r.at[i, k])

        def pstep(i, carry):
            rows = pl.ds(pl.multiple_of(i * TR, TR), TR)
            pre = dot(r.agg[rows, :], W[0], 1, 0) + dot(r.nf[rows, :], W[1], 1, 0)
            sg = 0.5 + 0.5 * jnp.tanh(0.5 * pre)
            gp = (r.cot[rows, :].astype(F32) * sg * (1.0 + pre * (1.0 - sg))).astype(BF)
            r.gp[rows, :] = gp
            gt = dot(W[0], gp, 1, 1).astype(BF)
            for t in range(TR // LANES):
                for c in range(NCH):
                    tile = gt[c * LANES : (c + 1) * LANES, t * LANES : (t + 1) * LANES]
                    r.gown[c, i * (TR // LANES) + t] = tile
                    gall[c][x * NB + i * (TR // LANES) + t] = tile
            for k in (1, 3):
                tile_send(i, k).start()
            return carry

        lax.fori_loop(0, NT, pstep, 0)

        NHB = NB // 2

        def xsend(c):
            for k in (1, 3):
                send(
                    r.gown.at[c], gall[c].at[pl.ds(x * NB, NB)], r.gs.at[c, k], r.gr.at[c, k], g, xdev(k)
                )

        def xforward(c):
            for k, off in ((1, 0), (3, NHB)):
                xs = (x - k + NX) % NX
                if c == 0:
                    for i in range(NT // 2):
                        tile_got(i + off // TB, k)
                else:
                    got(gall[c].at[pl.ds(xs * NB, NB)], r.gr.at[c, k])
                part = gall[c].at[pl.ds(xs * NB + off, NHB)]
                send(part, part, r.gs.at[c, 4 + k], r.gr.at[c, 4 + k], g, xdev(k))

        def xlast(c):
            xs = (x + 2) % NX
            if c == 0:
                for k, off in ((1, NHB), (3, 0)):
                    for i in range(NT // 2):
                        tile_got(i + off // TB, k)
            for k, off in ((1, 0), (3, NHB)):
                got(gall[c].at[pl.ds(xs * NB + off, NHB)], r.gr.at[c, 4 + k])

        def halo(c):
            def step(i, carry):
                for j in range(8):
                    s = i * 8 + j
                    r.hbuf[s] = dot(r.gown[c, r.htgt_s[s]], r.chalo[s], 1, 0)
                for j in range(8):
                    s = i * 8 + j
                    r.hbuf[s] = r.hbuf[s] + r.hbuf[r.hidx[s]]
                return carry

            lax.fori_loop(0, NH // 8, step, 0)
            for b in range(NB):
                r.hsend[c, b] = r.hbuf[r.hidx[NH + b]].astype(BF)
            send(r.hsend.at[c], r.hrecv.at[c], r.hs.at[c], r.hr.at[c], (g + 1) % NG, d)

        ring = r.ring

        def partial(c, zt):
            for s in range(NSL):
                r.ebuf[s] = dot(gall[c][r.idx[zt, s]], r.cin[s // CAP, zt, s % CAP], 1, 0)
            for s in range(1, NSL):
                r.ebuf[s] = r.ebuf[s] + r.ebuf[r.idx[zt, NSL + s]]

        def summed(zt, b):
            return r.ebuf[r.idx[zt, 2 * NSL + b]]

        def ring_step(c, q, dr, has_recv):
            dd = HALF - q
            sgn = 1 - 2 * dr
            zt = (z + sgn * dd + NZ) % NZ
            cgot((sgn * dd) % NZ)
            partial(c, zt)
            slot = ring.at[dr, c, q]
            if has_recv:
                got(slot, r.rr.at[dr, c, q])
                for b in range(NB):
                    ring[dr, c, q, b] = (summed(zt, b) + ring[dr, c, q, b].astype(F32)).astype(BF)
            else:
                for b in range(NB):
                    ring[dr, c, q, b] = summed(zt, b).astype(BF)
            nz = ((z + sgn + NZ) % NZ) * NX + x
            cp = rc(slot, ring.at[dr, c, q + 1], r.rs.at[dr, c, q], r.rr.at[dr, c, q + 1], g, nz)
            cp.start()
            pending.append(cp)

        class Reduce:
            def __init__(self, c):
                self.wp, self.ra, self.sa, self.rb = r.mwp.at[c], r.mra.at[c], r.msa.at[c], r.mrb.at[c]
                self.sb, self.rc, self.rd = r.msb.at[c], r.mrc.at[c], r.mrd.at[c]
                self.sem = r.msem.at[c]
                self.ni = 1

            def put(self, item, t):
                for yy in range(NY):
                    t4 = t[yy * TL * 16 : (yy + 1) * TL * 16].reshape(TL, 2, 8, LANES)
                    for hh in range(2):
                        self.wp[hh, yy, item] = t4[:, hh]

            def a_send(self):
                for k in range(1, NG):
                    gg = (g + k) % NG
                    send(self.wp.at[gg % 2, gg // 2], self.ra.at[k], self.sem.at[0, k], self.sem.at[1, k], gg, d)

            def a_sum_b_send(self):
                for k in range(1, NG):
                    got(self.ra.at[k], self.sem.at[1, k])

                def step(i, carry):
                    t = self.wp[h, y, i]
                    for k in range(1, NG):
                        t = t + self.ra[k, i]
                    t = t.reshape(ZZ, NX, 8, LANES)
                    for xx in range(NX):
                        self.sa[xx, i] = t[:, xx]
                    return carry

                lax.fori_loop(0, self.ni, step, 0)
                for k in range(1, NX):
                    send(self.sa.at[(x + k) % NX], self.rb.at[k], self.sem.at[2, k], self.sem.at[3, k], g, xdev(k))

            def b_sum_z_send(self):
                for k in range(1, NX):
                    got(self.rb.at[k], self.sem.at[3, k])

                def step(i, carry):
                    t = self.sa[x, i]
                    for k in range(1, NX):
                        t = t + self.rb[k, i]
                    for zi in range(ZZ):
                        self.sb[zi, i] = t[zi]
                    return carry

                lax.fori_loop(0, self.ni, step, 0)
                for zi in range(ZZ):
                    zd = y * ZZ + zi
                    k = (zd - z + NZ) % NZ

                    @pl.when(zd != z)
                    def _():
                        rc(
                            self.sb.at[zi], self.rc.at[k], self.sem.at[4, zi], self.sem.at[5, k], g, zd * NX + x
                        ).start()

            def z_sum_c_send(self):
                @pl.when(z // ZZ == y)
                def _():
                    for k in range(1, NZ):
                        got(self.rc.at[k], self.sem.at[5, k])

                    def step(i, carry):
                        t = self.sb[z % ZZ, i]
                        for k in range(1, NZ):
                            t = t + self.rc[k, i]
                        self.rd[h, i] = t
                        return carry

                    lax.fori_loop(0, self.ni, step, 0)
                    for k in range(1, NG):
                        rc(
                            self.rd.at[h], self.rd.at[h], self.sem.at[6, k], self.sem.at[7, h], (g + k) % NG, d
                        ).start()

            def finish(self, outs):
                @pl.when(z // ZZ == y)
                def _():
                    got(self.rd.at[1 - h], self.sem.at[7, 1 - h])
                    for k in range(1, NG):
                        rc(
                            self.rd.at[h], self.rd.at[h], self.sem.at[6, k], self.sem.at[7, h], (g + k) % NG, d
                        ).wait_send()

                @pl.when(z // ZZ != y)
                def _():
                    for hh in range(2):
                        got(self.rd.at[hh], self.sem.at[7, hh])

                for zi in range(ZZ):
                    zd = y * ZZ + zi

                    @pl.when(zd != z)
                    def _():
                        rc(
                            self.sb.at[zi], self.rc.at[0], self.sem.at[4, zi], self.sem.at[5, 0], g, zd * NX + x
                        ).wait_send()

                for i, (k, c) in enumerate(outs):
                    for hh in range(2):
                        r.gw_o[k, hh * 8 : hh * 8 + 8, c * LANES : (c + 1) * LANES] = self.rd[hh, i] * scale

        class ReduceItems:
            def a_send(self):
                for k in range(1, NG):
                    gg = (g + k) % NG
                    part = r.uwp.at[gg % 2, pl.ds((gg // 2) * IP, IP)]
                    send(part, r.ura.at[k], r.usem.at[0, k], r.usem.at[1, k], gg, d)

            def put(self, item, t):
                t4 = t.reshape(ND, 2, 8, LANES)
                for hh in range(2):
                    r.uwp[hh, item] = t4[:, hh]

            def a_sum_b_send(self):
                for k in range(1, NG):
                    got(r.ura.at[k], r.usem.at[1, k])

                def step(i, carry):
                    t = r.uwp[h, y * IP + i]
                    for k in range(1, NG):
                        t = t + r.ura[k, i]
                    t = t.reshape(NZ, NX, 8, LANES)
                    for xx in range(NX):
                        r.usa[xx, i] = t[:, xx]
                    return carry

                lax.fori_loop(0, IP, step, 0)
                for k in range(1, NX):
                    send(
                        r.usa.at[(x + k) % NX], r.urb.at[k], r.usem.at[2, k], r.usem.at[3, k], g, xdev(k)
                    )

            def b_sum_z_send(self):
                for k in range(1, NX):
                    got(r.urb.at[k], r.usem.at[3, k])
                for i in range(IP):
                    t = r.usa[x, i]
                    for k in range(1, NX):
                        t = t + r.urb[k, i]
                    for zd in range(NZ):
                        r.usb[zd, i] = t[zd]
                for k in range(1, NZ):
                    send(
                        r.usb.at[(z + k) % NZ], r.urc.at[k], r.usem.at[4, k], r.usem.at[5, k], g, zdev(k)
                    )

            def z_sum_c_send(self):
                for k in range(1, NZ):
                    got(r.urc.at[k], r.usem.at[5, k])
                for i in range(IP):
                    t = r.usb[z, i]
                    for k in range(1, NZ):
                        t = t + r.urc[k, i]
                    r.urd[h, y, i] = t
                part = r.urd.at[h, y]
                for k in range(1, NG):
                    send(part, part, r.usem.at[6, k], r.usem.at[7, k], (g + k) % NG, d)

            def finish(self, outs):
                for k in range(1, NG):
                    gg = (g - k + NG) % NG
                    got(r.urd.at[gg % 2, gg // 2], r.usem.at[7, k])
                for i, (k, c) in enumerate(outs):
                    for hh in range(2):
                        r.gw_o[k, hh * 8 : hh * 8 + 8, c * LANES : (c + 1) * LANES] = (
                            r.urd[hh, i // IP, i % IP] * scale
                        )

        red_u = ReduceItems()
        red_m = [Reduce(c) for c in range(NCH)]

        def own_grads():
            for c in range(NCH):
                cols = slice(c * LANES, (c + 1) * LANES)
                red_u.put(c, dot(r.agg[...], r.gp[:, cols], 0, 0))
                red_u.put(NCH + c, dot(r.nf[...], r.gp[:, cols], 0, 0))
            red_u.a_send()

        def final(c):
            cgot(0)
            partial(c, z)
            got(r.hrecv.at[c], r.hr.at[c])
            for dr in range(2):
                got(ring.at[dr, c, HALF], r.rr.at[dr, c, HALF])
            acc = jnp.zeros((LANES, D), F32)
            for b in range(NB):
                t = summed(z, b) + ring[0, c, HALF, b].astype(F32) + ring[1, c, HALF, b].astype(F32)
                t = t + jnp.where(g > 0, r.hrecv[c, b].astype(F32), 0.0)
                t = t.astype(BF)
                r.mt[c, b] = t
                acc = acc + dot(t, r.nf[b * LANES : (b + 1) * LANES, :], 1, 0)
            red_m[c].put(0, acc.T)
            red_m[c].a_send()

        def nodes_first():
            def step(i, carry):
                rows = pl.ds(pl.multiple_of(i * TR, TR), TR)
                r.gnacc[rows, :] = r.cot[rows, :].astype(F32) + dot(r.gp[rows, :], W[1], 1, 1)
                return carry

            lax.fori_loop(0, R // TR, step, 0)

        def nodes_add(cs, rows, b):
            t = r.gnacc[rows, :]
            per = NCH // 2
            for hh in range(2):
                mine = [c for c in cs if c // per == hh]
                if mine:
                    left = jnp.concatenate([r.mt[c, b].T for c in mine], axis=1)
                    lo = (mine[0] - hh * per) * LANES
                    t = t + dot(left, M[hh, :, lo : lo + len(mine) * LANES], 1, 1)
            return t

        def block_rows(b):
            return pl.ds(pl.multiple_of(b * LANES, LANES), LANES)

        def nodes_mid():
            for k in [0] + zorder:
                got(M.at[1 - h, zplane(k)], r.m3r.at[k])

            def step(b, carry):
                rows = block_rows(b)
                r.gnacc[rows, :] = nodes_add(range(NCH - 1), rows, b)
                return carry

            lax.fori_loop(0, NB, step, 0)

        def nodes_last():
            def step(b, carry):
                rows = block_rows(b)
                r.cot[rows, :] = nodes_add([NCH - 1], rows, b).astype(BF)
                return carry

            lax.fori_loop(0, NB, step, 0)
            load("out", r.cot, r.gn_o, 7)

        def weights_last():
            for k in zorder:
                got(M.at[h, zplane(k)], r.m2r.at[k])
                send(M.at[h, zplane(k)], M.at[h, zplane(k)], r.m3s.at[k], r.m3r.at[k], sib, d)

        xforward(0)
        if NCH > 1:
            xsend(1)
        halo(0)
        for w in range(NCH + HALF):
            chunks = [c for c in range(NCH) if 0 <= w - c < HALF]
            for c in chunks if w < 3 else chunks[::-1]:
                p = w - c
                if p == 0:
                    xlast(c)
                ring_step(c, p, c % 2, p > 0)
                if p + 1 < HALF:
                    ring_step(c, p + 1, 1 - c % 2, p > 0)
            if w + 1 < NCH:
                xforward(w + 1)
                if w + 2 < NCH:
                    xsend(w + 2)
            if w < 2:
                csend(1 - w)
            if w - HALF >= 0:
                final(w - HALF)
            if w == 0:
                weights_last()
            if w + 1 < NCH:
                halo(w + 1)
            if w == 1:
                own_grads()
            if w == 3:
                red_u.a_sum_b_send()
            if w == 4:
                red_u.b_sum_z_send()
                nodes_first()
            if w == 5:
                red_u.z_sum_c_send()
            if w == NCH + HALF - 2:
                nodes_mid()
            m = w - HALF
            if m >= 1:
                red_m[m - 1].a_sum_b_send()
            if m >= 2:
                red_m[m - 2].b_sum_z_send()
            if m >= 3:
                red_m[m - 3].z_sum_c_send()
        nodes_last()
        red_m[NCH - 1].a_sum_b_send()
        if NCH > 1:
            red_m[NCH - 2].b_sum_z_send()
        red_m[NCH - 1].b_sum_z_send()
        for m in range(max(NCH - 3, 0), NCH):
            red_m[m].z_sum_c_send()
        red_u.finish([(1, c) for c in range(NCH)] + [(2, c) for c in range(NCH)])
        for c in range(NCH):
            red_m[c].finish([(0, c)])
        for i in range(NT):
            for k in (1, 3):
                tile_send(i, k).wait_send()
        for cp in pending:
            cp.wait_send()
        loads["out"].wait()

    V = pltpu.VMEM
    S = pltpu.SMEM
    DMA = pltpu.SemaphoreType.DMA
    T2 = (LANES, LANES)
    scratch = [
        ("nf", V((R, D), BF)), ("agg", V((R, D), BF)), ("cot", V((R, D), BF)), ("gp", V((R, D), BF)),
        ("wst", V((2, 16, D), BF)), ("mst", V((2, 16, D // 2), BF)),
        ("W", V((2, D, D), BF)), ("M", V((2, D, D // 2), BF)),
        ("meta", V((8, LANES), jnp.int32)), ("mrecv", V((NX, 8, LANES), jnp.int32)), ("msm", S((NX, 8, LANES), jnp.int32)),
        ("idx", S((NZ, 2 * NSL + NB), jnp.int32)), ("hidx", S((NH + NB,), jnp.int32)),
        ("cin", V((NX, NZ, CAP) + T2, BF)), ("chalo", V((NH,) + T2, BF)),
        ("gown", V((NCH, NB) + T2, BF)),
        ("ebuf", V((NSL + 1,) + T2, F32)), ("hbuf", V((NH + 1,) + T2, F32)),
        ("hsend", V((NCH, NB) + T2, BF)), ("hrecv", V((NCH, NB) + T2, BF)),
        ("ring", V((2, NCH, HALF + 1, NB) + T2, BF)),
        ("mt", V((NCH, NB) + T2, BF)), ("gnacc", V((R, D), F32)),
    ]
    scratch += [
        ("uwp", V((2, NI, ND, 8, LANES), F32)), ("ura", V((NG, IP, ND, 8, LANES), F32)),
        ("usa", V((NX, IP, NZ, 8, LANES), F32)), ("urb", V((NX, IP, NZ, 8, LANES), F32)),
        ("usb", V((NZ, IP, 8, LANES), F32)), ("urc", V((NZ, IP, 8, LANES), F32)),
        ("urd", V((2, NY, IP, 8, LANES), F32)), ("usem", DMA((8, max(NG, NZ, NX)))),
    ]
    for n, lead, ni in (("m", (NCH,), 1),):
        scratch += [
            (n + "wp", V(lead + (2, NY, ni, TL, 8, LANES), F32)),
            (n + "ra", V(lead + (NG, ni, TL, 8, LANES), F32)),
            (n + "sa", V(lead + (NX, ni, ZZ, 8, LANES), F32)),
            (n + "rb", V(lead + (NX, ni, ZZ, 8, LANES), F32)),
            (n + "sb", V(lead + (ZZ, ni, 8, LANES), F32)),
            (n + "rc", V(lead + (NZ, ni, 8, LANES), F32)),
            (n + "rd", V(lead + (2, ni, 8, LANES), F32)),
            (n + "sem", DMA(lead + (8, max(NG, NZ, NX)))),
        ]
    scratch += [
        ("lsem", DMA((18,))),
        ("isrc_v", V((1, ND * CAP), jnp.int32)), ("itgt_v", V((1, ND * CAP), jnp.int32)),
        ("cnt_v", V((1, ND), jnp.int32)), ("own_s", S((1, ND * NB), jnp.int32)),
        ("hsrc_s", S((NH,), jnp.int32)), ("htgt_s", S((NH,), jnp.int32)),
        ("w1s", DMA((NX,))), ("w1r", DMA((NX,))), ("m1s", DMA((NX,))), ("m1r", DMA((NX,))),
        ("mts", DMA((NX,))), ("mtr", DMA((NX,))), ("cs", DMA((NZ, NX))), ("cr", DMA((NZ, NX))),
        ("w2s", DMA((NZ,))), ("w2r", DMA((NZ,))), ("w3s", DMA((NZ,))), ("w3r", DMA((NZ,))),
        ("m2s", DMA((NZ,))), ("m2r", DMA((NZ,))), ("m3s", DMA((NZ,))), ("m3r", DMA((NZ,))),
        ("g0s", DMA((R // TR, NX))), ("g0r", DMA((R // TR, NX))), ("gs", DMA((NCH, 8))), ("gr", DMA((NCH, 8))),
        ("rs", DMA((2, NCH, HALF))), ("rr", DMA((2, NCH, HALF + 1))),
        ("hs", DMA((NCH,))), ("hr", DMA((NCH,))),
        ("wys", DMA((NY, NZ))), ("wyr", DMA((NY, NZ))), ("wbs", DMA((NY,))), ("wbr", DMA((NY,))),
    ]
    scratch += [("g%d" % c, V((NX * NB + 1,) + T2, BF)) for c in range(NCH)]
    any_, vm = (pl.BlockSpec(memory_space=m) for m in (pl.ANY, pltpu.VMEM))
    return pl.pallas_call(
        kernel,
        out_shape=(jax.ShapeDtypeStruct((R, D), BF), jax.ShapeDtypeStruct((3, 16, D), F32)),
        in_specs=[any_] * 14,
        out_specs=(any_, vm),
        scratch_shapes=[s for _, s in scratch],
        compiler_params=pltpu.CompilerParams(
            collective_id=0, has_side_effects=True, vmem_limit_bytes=56 * 1024 * 1024
        ),
        cost_estimate=pl.CostEstimate(flops=8 * 10**9, bytes_accessed=10**7, transcendentals=R * D),
    )


def local(
    node_feats,
    aggregate,
    cotangent,
    msg_weight,
    upd_weight,
    self_weight,
    owner_map,
    inner_source,
    inner_target,
    inner_contact,
    send_counts,
    halo_source,
    halo_target,
    halo_contact,
):
    R, D = node_feats.shape
    NG, ND = lax.axis_size("group"), lax.axis_size("dev")
    NZ = ND // NX
    cap = inner_source.shape[0] // ND
    nb = R // LANES

    run = make_kernel(NG, ND, R, D, nb, cap, halo_source.shape[0], 1.0 / math.sqrt(R * ND * NG))
    gn, gw = run(
        node_feats, aggregate, cotangent, msg_weight, upd_weight, self_weight, owner_map,
        inner_source.reshape(1, -1), inner_target.reshape(1, -1), send_counts, halo_source, halo_target, inner_contact.reshape(NZ, NX, cap, LANES, LANES), halo_contact,
    )
    return gn, gw[0], gw[1], gw[2]


def solution(mesh):
    both = ("group", "dev")
    in_specs = (
        P(both, None), P(both, None), P(both, None), P("dev", None), P("dev", None), P("dev", None),
        P("group", None), P(both), P(both), P(both, None, None), P(both, None), P(both), P(both),
        P(both, None, None),
    )
    out_specs = (P(both, None), P("dev", None), P("dev", None), P("dev", None))
    return jax.shard_map(local, mesh=mesh, in_specs=in_specs, out_specs=out_specs, check_vma=False)
```

```python
import math
from types import SimpleNamespace

import jax
import jax.numpy as jnp
from jax import lax
from jax.experimental import pallas as pl
from jax.experimental.pallas import tpu as pltpu
from jax.sharding import PartitionSpec as P

BF = jnp.bfloat16
F32 = jnp.float32
NX = 4
LANES = 128
MESH = pl.DeviceIdType.MESH


def dot(a, b, ca, cb):
    return lax.dot_general(a, b, (((ca,), (cb,)), ((), ())), preferred_element_type=F32)


def make_kernel(NG, ND, R, D, NB, CAP, NH, scale):
    NZ = ND // NX
    NY = NG // 2
    ZZ = NZ // NY
    NCH = D // LANES
    NSL = NX * CAP
    HALF = NZ // 2
    TR = min(256, R)
    NI = 2 * NCH
    TL = ZZ * NX
    ZROW = NX * 16
    LY = D // NY
    IP = NI // NY

    def kernel(*refs):
        names = [
            "nf_h", "agg_h", "cot_h", "msg_h", "upd_h", "self_h", "own_h", "isrc_h", "itgt_h", "cnt_h", "hsrc_h", "htgt_h",
            "inner_h", "halo_h", "gn_o", "gw_o",
        ] + [n for n, _ in scratch]
        r = SimpleNamespace(**dict(zip(names, refs)))
        gall = refs[-NCH:]
        g = lax.axis_index("group")
        d = lax.axis_index("dev")
        y, h = g // 2, g % 2
        z, x = d // NX, d % NX
        sib = y * 2 + (1 - h)

        def xdev(k):
            return z * NX + (x + k) % NX

        def zdev(k):
            return ((z + k + NZ) % NZ) * NX + x

        def rc(src, dst, ss, rs, gg, dd):
            return pltpu.make_async_remote_copy(
                src_ref=src, dst_ref=dst, send_sem=ss, recv_sem=rs, device_id=(gg, dd), device_id_type=MESH
            )

        pending = []

        def send(src, dst, ss, rs, gg, dd):
            cp = rc(src, dst, ss, rs, gg, dd)
            cp.start()
            pending.append(cp)

        def got(dst, rs):
            rc(dst, dst, rs, rs, sib, d).wait_recv()

        bar = pltpu.get_barrier_semaphore()

        def greet(gg, dd):
            pl.semaphore_signal(bar, inc=1, device_id=(gg, dd), device_id_type=MESH)

        for k in range(1, NX):
            greet(g, xdev(k))
        for k in range(1, NZ):
            greet(g, zdev(k))
        for k in range(1, NG):
            greet((g + k) % NG, d)

        loads = {}

        def load(name, src, dst, i):
            cp = pltpu.make_async_copy(src, dst, r.lsem.at[i])
            cp.start()
            loads[name] = cp

        HD = D // 2
        load("upd", r.upd_h, r.wst.at[0], 0)
        load("self", r.self_h, r.wst.at[1], 1)
        load("isrc", r.isrc_h, r.isrc_v, 12)
        load("itgt", r.itgt_h, r.itgt_v, 13)
        load("cnt", r.cnt_h, r.cnt_v, 14)
        load("m0", r.msg_h.at[:, pl.ds(0, HD)], r.mst.at[0], 2)
        load("m1", r.msg_h.at[:, pl.ds(HD, HD)], r.mst.at[1], 3)

        load("own", r.own_h, r.own_s, 15)
        load("hsrc", r.hsrc_h, r.hsrc_s, 16)
        load("htgt", r.htgt_h, r.htgt_s, 17)
        load("agg", r.agg_h, r.agg, 8)
        load("nf", r.nf_h, r.nf, 9)
        load("cot", r.cot_h, r.cot, 10)
        load("halo", r.halo_h, r.chalo, 11)
        load("cin", r.inner_h.at[:, x], r.cin.at[x], 4)

        zero = jnp.zeros((LANES, LANES), F32)
        r.ebuf[NSL] = zero
        r.hbuf[NH] = zero
        for c in range(NCH):
            gall[c][NX * NB] = zero.astype(BF)
        for n in ("upd", "self", "m0", "m1", "isrc", "itgt", "cnt"):
            loads[n].wait()
        W, M = r.W, r.M
        row0 = pl.multiple_of(d * 16, 16)
        plane = pl.ds(pl.multiple_of(z * ZROW, 16), ZROW)
        M[h, pl.ds(row0, 16), :] = r.mst[h]
        r.meta[0:1, 0 : ND * CAP] = r.isrc_v[...]
        r.meta[1:2, 0 : ND * CAP] = r.itgt_v[...]
        r.meta[2:3, 0:ND] = r.cnt_v[...]
        r.mrecv[x] = r.meta[...]
        pl.semaphore_wait(bar, NX - 1 + NZ - 1 + NG - 1)

        myrow = pl.ds(row0, 16)

        def lanes(j):
            return pl.ds(pl.multiple_of(((y - j + NY) % NY) * LY, LANES), LY)

        def wpart(core, rows, j):
            return W.at[core, rows, lanes(j)]

        for k in (1, 3, 2):
            send(r.wst.at[h, :, lanes(0)], wpart(h, myrow, 0), r.w1s.at[k], r.w1r.at[k], g, xdev(k))
        load("w", r.wst.at[h, :, lanes(0)], wpart(h, myrow, 0), 6)
        for k in (1, 3, 2):
            send(r.mst.at[h], M.at[h, myrow], r.m1s.at[k], r.m1r.at[k], g, xdev(k))
            send(r.meta, r.mrecv.at[x], r.mts.at[k], r.mtr.at[k], g, xdev(k))

        def csend(dd):
            for off in sorted({dd % NZ, (NZ - dd) % NZ}):
                zt = (z + off) % NZ
                for k in (1, 3, 2):
                    send(
                        r.inner_h.at[zt, (x + k) % NX], r.cin.at[x, zt], r.cs.at[off, k], r.cr.at[off, k],
                        g, xdev(k),
                    )

        have = set()

        def cgot(off):
            if off in have:
                return
            have.add(off)
            zt = (z + off) % NZ
            for k in (1, 3, 2):
                got(r.cin.at[(x - k + NX) % NX, zt], r.cr.at[off, k])

        for k in (1, 3, 2):
            got(wpart(h, myrow, 0), r.w1r.at[k])
        loads["w"].wait()
        zorder = sorted(range(1, NZ), key=lambda k: min(k, NZ - k))

        def zplane(k):
            return pl.ds(pl.multiple_of(((z - k + NZ) % NZ) * ZROW, 16), ZROW)

        def hand_on(k):
            part = wpart(h, zplane(k), 0)
            for j in range(1, NY):
                send(part, part, r.wys.at[j, k], r.wyr.at[j, k], ((y + j) % NY) * 2 + h, d)
            send(part, part, r.w3s.at[k], r.w3r.at[k], sib, d)

        for k in zorder[::-1]:
            part = wpart(h, plane, 0)
            send(part, part, r.w2s.at[k], r.w2r.at[k], g, zdev(k))
        hand_on(0)
        for dd in range(HALF, 1, -1):
            csend(dd)
        for k in (1, 3, 2):
            got(M.at[h, myrow], r.m1r.at[k])
            got(r.mrecv.at[x], r.mtr.at[k])
        meta_in = pltpu.make_async_copy(r.mrecv, r.msm, r.lsem.at[5])
        meta_in.start()
        def hstep(s, last):
            src = r.hsrc_s[s]
            prev = jnp.int32(NH)
            for b in range(NB):
                prev = jnp.where(src == b, last[b], prev)
            r.hidx[s] = prev
            return tuple(jnp.where(src == b, s, last[b]) for b in range(NB))


        for n in ("own", "hsrc", "htgt"):
            loads[n].wait()
        last = lax.fori_loop(0, NH, hstep, (jnp.int32(NH),) * NB)
        for b in range(NB):
            r.hidx[NH + b] = last[b]

        for k in zorder:
            got(wpart(h, zplane(k), 0), r.w2r.at[k])
            hand_on(k)
        for k in range(1, NZ):
            send(M.at[h, plane], M.at[h, plane], r.m2s.at[k], r.m2r.at[k], g, zdev(k))
        send(M.at[h, plane], M.at[h, plane], r.m3s.at[0], r.m3r.at[0], sib, d)

        def istep(zt, carry):
            dst = []
            for s in range(NSL):
                xs, cc = s // CAP, s % CAP
                peer = zt * NX + x
                dst.append(lax.rem(r.own_s[0, r.msm[xs, 0, peer * CAP + cc]], NB))
                r.idx[zt, s] = jnp.where(
                    cc < r.msm[xs, 2, peer], xs * NB + r.msm[xs, 1, peer * CAP + cc], NX * NB
                )
            for s in range(NSL):
                p = jnp.int32(NSL)
                for j in range(s):
                    p = jnp.where(dst[j] == dst[s], j, p)
                r.idx[zt, NSL + s] = p
            for b in range(NB):
                p = jnp.int32(NSL)
                for j in range(NSL):
                    p = jnp.where(dst[j] == b, j, p)
                r.idx[zt, 2 * NSL + b] = p
            return carry

        meta_in.wait()
        lax.fori_loop(0, NZ, istep, 0)

        for j in range(1, NY):
            for k in [0] + zorder:
                got(wpart(h, zplane(k), j), r.wyr.at[j, k])
            part = wpart(h, pl.ds(0, D), j)
            send(part, part, r.wbs.at[j], r.wbr.at[j], sib, d)
        for k in [0] + zorder:
            got(wpart(1 - h, zplane(k), 0), r.w3r.at[k])
        for j in range(1, NY):
            got(wpart(1 - h, pl.ds(0, D), j), r.wbr.at[j])
        for n in ("agg", "nf", "cot", "halo", "cin"):
            loads[n].wait()

        NT = R // TR
        TB = TR // LANES

        def tile_send(i, k):
            return rc(
                r.gown.at[0, pl.ds(i * TB, TB)], gall[0].at[pl.ds(x * NB + i * TB, TB)],
                r.g0s.at[i, k], r.g0r.at[i, k], g, xdev(k),
            )

        def tile_got(i, k):
            got(gall[0].at[pl.ds((x - k + NX) % NX * NB + i * TB, TB)], r.g0r.at[i, k])

        def pstep(i, carry):
            rows = pl.ds(pl.multiple_of(i * TR, TR), TR)
            pre = dot(r.agg[rows, :], W[0], 1, 0) + dot(r.nf[rows, :], W[1], 1, 0)
            sg = 0.5 + 0.5 * jnp.tanh(0.5 * pre)
            gp = (r.cot[rows, :].astype(F32) * sg * (1.0 + pre * (1.0 - sg))).astype(BF)
            r.gp[rows, :] = gp
            gt = dot(W[0], gp, 1, 1).astype(BF)
            for t in range(TR // LANES):
                for c in range(NCH):
                    tile = gt[c * LANES : (c + 1) * LANES, t * LANES : (t + 1) * LANES]
                    r.gown[c, i * (TR // LANES) + t] = tile
                    gall[c][x * NB + i * (TR // LANES) + t] = tile
            for k in (1, 3):
                tile_send(i, k).start()
            return carry

        lax.fori_loop(0, NT, pstep, 0)

        NHB = NB // 2

        def xsend(c):
            for k in (1, 3):
                send(
                    r.gown.at[c], gall[c].at[pl.ds(x * NB, NB)], r.gs.at[c, k], r.gr.at[c, k], g, xdev(k)
                )

        def xforward(c):
            for k, off in ((1, 0), (3, NHB)):
                xs = (x - k + NX) % NX
                if c == 0:
                    for i in range(NT // 2):
                        tile_got(i + off // TB, k)
                else:
                    got(gall[c].at[pl.ds(xs * NB, NB)], r.gr.at[c, k])
                part = gall[c].at[pl.ds(xs * NB + off, NHB)]
                send(part, part, r.gs.at[c, 4 + k], r.gr.at[c, 4 + k], g, xdev(k))

        def xlast(c):
            xs = (x + 2) % NX
            if c == 0:
                for k, off in ((1, NHB), (3, 0)):
                    for i in range(NT // 2):
                        tile_got(i + off // TB, k)
            for k, off in ((1, 0), (3, NHB)):
                got(gall[c].at[pl.ds(xs * NB + off, NHB)], r.gr.at[c, 4 + k])

        def halo(c):
            def step(i, carry):
                for j in range(8):
                    s = i * 8 + j
                    r.hbuf[s] = dot(r.gown[c, r.htgt_s[s]], r.chalo[s], 1, 0)
                for j in range(8):
                    s = i * 8 + j
                    r.hbuf[s] = r.hbuf[s] + r.hbuf[r.hidx[s]]
                return carry

            lax.fori_loop(0, NH // 8, step, 0)
            for b in range(NB):
                r.hsend[c, b] = r.hbuf[r.hidx[NH + b]].astype(BF)
            send(r.hsend.at[c], r.hrecv.at[c], r.hs.at[c], r.hr.at[c], (g + 1) % NG, d)

        ring = r.ring

        def partial(c, zt):
            for s in range(NSL):
                r.ebuf[s] = dot(gall[c][r.idx[zt, s]], r.cin[s // CAP, zt, s % CAP], 1, 0)
            for s in range(1, NSL):
                r.ebuf[s] = r.ebuf[s] + r.ebuf[r.idx[zt, NSL + s]]

        def summed(zt, b):
            return r.ebuf[r.idx[zt, 2 * NSL + b]]

        def ring_step(c, q, dr, has_recv):
            dd = HALF - q
            sgn = 1 - 2 * dr
            zt = (z + sgn * dd + NZ) % NZ
            cgot((sgn * dd) % NZ)
            partial(c, zt)
            slot = ring.at[dr, c, q]
            if has_recv:
                got(slot, r.rr.at[dr, c, q])
                for b in range(NB):
                    ring[dr, c, q, b] = (summed(zt, b) + ring[dr, c, q, b].astype(F32)).astype(BF)
            else:
                for b in range(NB):
                    ring[dr, c, q, b] = summed(zt, b).astype(BF)
            nz = ((z + sgn + NZ) % NZ) * NX + x
            cp = rc(slot, ring.at[dr, c, q + 1], r.rs.at[dr, c, q], r.rr.at[dr, c, q + 1], g, nz)
            cp.start()
            pending.append(cp)

        class Reduce:
            def __init__(self, c):
                self.wp, self.ra, self.sa, self.rb = r.mwp.at[c], r.mra.at[c], r.msa.at[c], r.mrb.at[c]
                self.sb, self.rc, self.rd = r.msb.at[c], r.mrc.at[c], r.mrd.at[c]
                self.sem = r.msem.at[c]
                self.ni = 1

            def put(self, item, t):
                for yy in range(NY):
                    t4 = t[yy * TL * 16 : (yy + 1) * TL * 16].reshape(TL, 2, 8, LANES)
                    for hh in range(2):
                        self.wp[hh, yy, item] = t4[:, hh]

            def a_send(self):
                for k in range(1, NG):
                    gg = (g + k) % NG
                    send(self.wp.at[gg % 2, gg // 2], self.ra.at[k], self.sem.at[0, k], self.sem.at[1, k], gg, d)

            def a_sum_b_send(self):
                for k in range(1, NG):
                    got(self.ra.at[k], self.sem.at[1, k])

                def step(i, carry):
                    t = self.wp[h, y, i]
                    for k in range(1, NG):
                        t = t + self.ra[k, i]
                    t = t.reshape(ZZ, NX, 8, LANES)
                    for xx in range(NX):
                        self.sa[xx, i] = t[:, xx]
                    return carry

                lax.fori_loop(0, self.ni, step, 0)
                for k in range(1, NX):
                    send(self.sa.at[(x + k) % NX], self.rb.at[k], self.sem.at[2, k], self.sem.at[3, k], g, xdev(k))

            def b_sum_z_send(self):
                for k in range(1, NX):
                    got(self.rb.at[k], self.sem.at[3, k])

                def step(i, carry):
                    t = self.sa[x, i]
                    for k in range(1, NX):
                        t = t + self.rb[k, i]
                    for zi in range(ZZ):
                        self.sb[zi, i] = t[zi]
                    return carry

                lax.fori_loop(0, self.ni, step, 0)
                for zi in range(ZZ):
                    zd = y * ZZ + zi
                    k = (zd - z + NZ) % NZ

                    @pl.when(zd != z)
                    def _():
                        rc(
                            self.sb.at[zi], self.rc.at[k], self.sem.at[4, zi], self.sem.at[5, k], g, zd * NX + x
                        ).start()

            def z_sum_c_send(self):
                @pl.when(z // ZZ == y)
                def _():
                    for k in range(1, NZ):
                        got(self.rc.at[k], self.sem.at[5, k])

                    def step(i, carry):
                        t = self.sb[z % ZZ, i]
                        for k in range(1, NZ):
                            t = t + self.rc[k, i]
                        self.rd[h, i] = t
                        return carry

                    lax.fori_loop(0, self.ni, step, 0)
                    for k in range(1, NG):
                        rc(
                            self.rd.at[h], self.rd.at[h], self.sem.at[6, k], self.sem.at[7, h], (g + k) % NG, d
                        ).start()

            def finish(self, outs):
                @pl.when(z // ZZ == y)
                def _():
                    got(self.rd.at[1 - h], self.sem.at[7, 1 - h])
                    for k in range(1, NG):
                        rc(
                            self.rd.at[h], self.rd.at[h], self.sem.at[6, k], self.sem.at[7, h], (g + k) % NG, d
                        ).wait_send()

                @pl.when(z // ZZ != y)
                def _():
                    for hh in range(2):
                        got(self.rd.at[hh], self.sem.at[7, hh])

                for zi in range(ZZ):
                    zd = y * ZZ + zi

                    @pl.when(zd != z)
                    def _():
                        rc(
                            self.sb.at[zi], self.rc.at[0], self.sem.at[4, zi], self.sem.at[5, 0], g, zd * NX + x
                        ).wait_send()

                for i, (k, c) in enumerate(outs):
                    for hh in range(2):
                        r.gw_o[k, hh * 8 : hh * 8 + 8, c * LANES : (c + 1) * LANES] = self.rd[hh, i] * scale

        class ReduceItems:
            def a_send(self):
                for k in range(1, NG):
                    gg = (g + k) % NG
                    part = r.uwp.at[gg % 2, pl.ds((gg // 2) * IP, IP)]
                    send(part, r.ura.at[k], r.usem.at[0, k], r.usem.at[1, k], gg, d)

            def put(self, item, t):
                t4 = t.reshape(ND, 2, 8, LANES)
                for hh in range(2):
                    r.uwp[hh, item] = t4[:, hh]

            def a_sum_b_send(self):
                for k in range(1, NG):
                    got(r.ura.at[k], r.usem.at[1, k])

                def step(i, carry):
                    t = r.uwp[h, y * IP + i]
                    for k in range(1, NG):
                        t = t + r.ura[k, i]
                    t = t.reshape(NZ, NX, 8, LANES)
                    for xx in range(NX):
                        r.usa[xx, i] = t[:, xx]
                    return carry

                lax.fori_loop(0, IP, step, 0)
                for k in range(1, NX):
                    send(
                        r.usa.at[(x + k) % NX], r.urb.at[k], r.usem.at[2, k], r.usem.at[3, k], g, xdev(k)
                    )

            def b_sum_z_send(self):
                for k in range(1, NX):
                    got(r.urb.at[k], r.usem.at[3, k])
                for i in range(IP):
                    t = r.usa[x, i]
                    for k in range(1, NX):
                        t = t + r.urb[k, i]
                    for zd in range(NZ):
                        r.usb[zd, i] = t[zd]
                for k in range(1, NZ):
                    send(
                        r.usb.at[(z + k) % NZ], r.urc.at[k], r.usem.at[4, k], r.usem.at[5, k], g, zdev(k)
                    )

            def z_sum_c_send(self):
                for k in range(1, NZ):
                    got(r.urc.at[k], r.usem.at[5, k])
                for i in range(IP):
                    t = r.usb[z, i]
                    for k in range(1, NZ):
                        t = t + r.urc[k, i]
                    r.urd[h, y, i] = t
                part = r.urd.at[h, y]
                for k in range(1, NG):
                    send(part, part, r.usem.at[6, k], r.usem.at[7, k], (g + k) % NG, d)

            def finish(self, outs):
                for k in range(1, NG):
                    gg = (g - k + NG) % NG
                    got(r.urd.at[gg % 2, gg // 2], r.usem.at[7, k])
                for i, (k, c) in enumerate(outs):
                    for hh in range(2):
                        r.gw_o[k, hh * 8 : hh * 8 + 8, c * LANES : (c + 1) * LANES] = (
                            r.urd[hh, i // IP, i % IP] * scale
                        )

        red_u = ReduceItems()
        red_m = [Reduce(c) for c in range(NCH)]

        def own_grads():
            for c in range(NCH):
                cols = slice(c * LANES, (c + 1) * LANES)
                red_u.put(c, dot(r.agg[...], r.gp[:, cols], 0, 0))
                red_u.put(NCH + c, dot(r.nf[...], r.gp[:, cols], 0, 0))
            red_u.a_send()

        def final(c):
            cgot(0)
            partial(c, z)
            got(r.hrecv.at[c], r.hr.at[c])
            for dr in range(2):
                got(ring.at[dr, c, HALF], r.rr.at[dr, c, HALF])
            acc = jnp.zeros((LANES, D), F32)
            for b in range(NB):
                t = summed(z, b) + ring[0, c, HALF, b].astype(F32) + ring[1, c, HALF, b].astype(F32)
                t = t + jnp.where(g > 0, r.hrecv[c, b].astype(F32), 0.0)
                t = t.astype(BF)
                r.mt[c, b] = t
                acc = acc + dot(t, r.nf[b * LANES : (b + 1) * LANES, :], 1, 0)
            red_m[c].put(0, acc.T)
            red_m[c].a_send()

        def nodes_first():
            def step(i, carry):
                rows = pl.ds(pl.multiple_of(i * TR, TR), TR)
                r.gnacc[rows, :] = r.cot[rows, :].astype(F32) + dot(r.gp[rows, :], W[1], 1, 1)
                return carry

            lax.fori_loop(0, R // TR, step, 0)

        def nodes_add(cs, rows, b):
            t = r.gnacc[rows, :]
            per = NCH // 2
            for hh in range(2):
                mine = [c for c in cs if c // per == hh]
                if mine:
                    left = jnp.concatenate([r.mt[c, b].T for c in mine], axis=1)
                    lo = (mine[0] - hh * per) * LANES
                    t = t + dot(left, M[hh, :, lo : lo + len(mine) * LANES], 1, 1)
            return t

        def block_rows(b):
            return pl.ds(pl.multiple_of(b * LANES, LANES), LANES)

        def nodes_mid():
            for k in [0] + zorder:
                got(M.at[1 - h, zplane(k)], r.m3r.at[k])

            def step(b, carry):
                rows = block_rows(b)
                r.gnacc[rows, :] = nodes_add(range(NCH // 2), rows, b)
                return carry

            lax.fori_loop(0, NB, step, 0)

        def nodes_last():
            def step(b, carry):
                rows = block_rows(b)
                r.cot[rows, :] = nodes_add(range(NCH // 2, NCH), rows, b).astype(BF)
                return carry

            lax.fori_loop(0, NB, step, 0)
            load("out", r.cot, r.gn_o, 7)

        def weights_last():
            for k in zorder:
                got(M.at[h, zplane(k)], r.m2r.at[k])
                send(M.at[h, zplane(k)], M.at[h, zplane(k)], r.m3s.at[k], r.m3r.at[k], sib, d)

        xforward(0)
        if NCH > 1:
            xsend(1)
        halo(0)
        for w in range(NCH + HALF):
            chunks = [c for c in range(NCH) if 0 <= w - c < HALF]
            for c in chunks if w < 3 else chunks[::-1]:
                p = w - c
                if p == 0:
                    xlast(c)
                ring_step(c, p, c % 2, p > 0)
                if p + 1 < HALF:
                    ring_step(c, p + 1, 1 - c % 2, p > 0)
            if w + 1 < NCH:
                xforward(w + 1)
                if w + 2 < NCH:
                    xsend(w + 2)
            if w < 2:
                csend(1 - w)
            if w - HALF >= 0:
                final(w - HALF)
            if w == 0:
                weights_last()
            if w + 1 < NCH:
                halo(w + 1)
            if w == 1:
                own_grads()
            if w == 3:
                red_u.a_sum_b_send()
            if w == 4:
                red_u.b_sum_z_send()
                nodes_first()
            if w == 5:
                red_u.z_sum_c_send()
            if w == NCH + HALF - 3:
                nodes_mid()
            m = w - HALF
            if m >= 1:
                red_m[m - 1].a_sum_b_send()
            if m >= 2:
                red_m[m - 2].b_sum_z_send()
            if m >= 3:
                red_m[m - 3].z_sum_c_send()
        nodes_last()
        red_m[NCH - 1].a_sum_b_send()
        if NCH > 1:
            red_m[NCH - 2].b_sum_z_send()
        red_m[NCH - 1].b_sum_z_send()
        for m in range(max(NCH - 3, 0), NCH):
            red_m[m].z_sum_c_send()
        red_u.finish([(1, c) for c in range(NCH)] + [(2, c) for c in range(NCH)])
        for c in range(NCH):
            red_m[c].finish([(0, c)])
        for i in range(NT):
            for k in (1, 3):
                tile_send(i, k).wait_send()
        for cp in pending:
            cp.wait_send()
        loads["out"].wait()

    V = pltpu.VMEM
    S = pltpu.SMEM
    DMA = pltpu.SemaphoreType.DMA
    T2 = (LANES, LANES)
    scratch = [
        ("nf", V((R, D), BF)), ("agg", V((R, D), BF)), ("cot", V((R, D), BF)), ("gp", V((R, D), BF)),
        ("wst", V((2, 16, D), BF)), ("mst", V((2, 16, D // 2), BF)),
        ("W", V((2, D, D), BF)), ("M", V((2, D, D // 2), BF)),
        ("meta", V((8, LANES), jnp.int32)), ("mrecv", V((NX, 8, LANES), jnp.int32)), ("msm", S((NX, 8, LANES), jnp.int32)),
        ("idx", S((NZ, 2 * NSL + NB), jnp.int32)), ("hidx", S((NH + NB,), jnp.int32)),
        ("cin", V((NX, NZ, CAP) + T2, BF)), ("chalo", V((NH,) + T2, BF)),
        ("gown", V((NCH, NB) + T2, BF)),
        ("ebuf", V((NSL + 1,) + T2, F32)), ("hbuf", V((NH + 1,) + T2, F32)),
        ("hsend", V((NCH, NB) + T2, BF)), ("hrecv", V((NCH, NB) + T2, BF)),
        ("ring", V((2, NCH, HALF + 1, NB) + T2, BF)),
        ("mt", V((NCH, NB) + T2, BF)), ("gnacc", V((R, D), F32)),
    ]
    scratch += [
        ("uwp", V((2, NI, ND, 8, LANES), F32)), ("ura", V((NG, IP, ND, 8, LANES), F32)),
        ("usa", V((NX, IP, NZ, 8, LANES), F32)), ("urb", V((NX, IP, NZ, 8, LANES), F32)),
        ("usb", V((NZ, IP, 8, LANES), F32)), ("urc", V((NZ, IP, 8, LANES), F32)),
        ("urd", V((2, NY, IP, 8, LANES), F32)), ("usem", DMA((8, max(NG, NZ, NX)))),
    ]
    for n, lead, ni in (("m", (NCH,), 1),):
        scratch += [
            (n + "wp", V(lead + (2, NY, ni, TL, 8, LANES), F32)),
            (n + "ra", V(lead + (NG, ni, TL, 8, LANES), F32)),
            (n + "sa", V(lead + (NX, ni, ZZ, 8, LANES), F32)),
            (n + "rb", V(lead + (NX, ni, ZZ, 8, LANES), F32)),
            (n + "sb", V(lead + (ZZ, ni, 8, LANES), F32)),
            (n + "rc", V(lead + (NZ, ni, 8, LANES), F32)),
            (n + "rd", V(lead + (2, ni, 8, LANES), F32)),
            (n + "sem", DMA(lead + (8, max(NG, NZ, NX)))),
        ]
    scratch += [
        ("lsem", DMA((18,))),
        ("isrc_v", V((1, ND * CAP), jnp.int32)), ("itgt_v", V((1, ND * CAP), jnp.int32)),
        ("cnt_v", V((1, ND), jnp.int32)), ("own_s", S((1, ND * NB), jnp.int32)),
        ("hsrc_s", S((NH,), jnp.int32)), ("htgt_s", S((NH,), jnp.int32)),
        ("w1s", DMA((NX,))), ("w1r", DMA((NX,))), ("m1s", DMA((NX,))), ("m1r", DMA((NX,))),
        ("mts", DMA((NX,))), ("mtr", DMA((NX,))), ("cs", DMA((NZ, NX))), ("cr", DMA((NZ, NX))),
        ("w2s", DMA((NZ,))), ("w2r", DMA((NZ,))), ("w3s", DMA((NZ,))), ("w3r", DMA((NZ,))),
        ("m2s", DMA((NZ,))), ("m2r", DMA((NZ,))), ("m3s", DMA((NZ,))), ("m3r", DMA((NZ,))),
        ("g0s", DMA((R // TR, NX))), ("g0r", DMA((R // TR, NX))), ("gs", DMA((NCH, 8))), ("gr", DMA((NCH, 8))),
        ("rs", DMA((2, NCH, HALF))), ("rr", DMA((2, NCH, HALF + 1))),
        ("hs", DMA((NCH,))), ("hr", DMA((NCH,))),
        ("wys", DMA((NY, NZ))), ("wyr", DMA((NY, NZ))), ("wbs", DMA((NY,))), ("wbr", DMA((NY,))),
    ]
    scratch += [("g%d" % c, V((NX * NB + 1,) + T2, BF)) for c in range(NCH)]
    any_, vm = (pl.BlockSpec(memory_space=m) for m in (pl.ANY, pltpu.VMEM))
    return pl.pallas_call(
        kernel,
        out_shape=(jax.ShapeDtypeStruct((R, D), BF), jax.ShapeDtypeStruct((3, 16, D), F32)),
        in_specs=[any_] * 14,
        out_specs=(any_, vm),
        scratch_shapes=[s for _, s in scratch],
        compiler_params=pltpu.CompilerParams(
            collective_id=0, has_side_effects=True, vmem_limit_bytes=56 * 1024 * 1024
        ),
        cost_estimate=pl.CostEstimate(flops=8 * 10**9, bytes_accessed=10**7, transcendentals=R * D),
    )


def local(
    node_feats,
    aggregate,
    cotangent,
    msg_weight,
    upd_weight,
    self_weight,
    owner_map,
    inner_source,
    inner_target,
    inner_contact,
    send_counts,
    halo_source,
    halo_target,
    halo_contact,
):
    R, D = node_feats.shape
    NG, ND = lax.axis_size("group"), lax.axis_size("dev")
    NZ = ND // NX
    cap = inner_source.shape[0] // ND
    nb = R // LANES

    run = make_kernel(NG, ND, R, D, nb, cap, halo_source.shape[0], 1.0 / math.sqrt(R * ND * NG))
    gn, gw = run(
        node_feats, aggregate, cotangent, msg_weight, upd_weight, self_weight, owner_map,
        inner_source.reshape(1, -1), inner_target.reshape(1, -1), send_counts, halo_source, halo_target, inner_contact.reshape(NZ, NX, cap, LANES, LANES), halo_contact,
    )
    return gn, gw[0], gw[1], gw[2]


def solution(mesh):
    both = ("group", "dev")
    in_specs = (
        P(both, None), P(both, None), P(both, None), P("dev", None), P("dev", None), P("dev", None),
        P("group", None), P(both), P(both), P(both, None, None), P(both, None), P(both), P(both),
        P(both, None, None),
    )
    out_specs = (P(both, None), P("dev", None), P("dev", None), P("dev", None))
    return jax.shard_map(local, mesh=mesh, in_specs=in_specs, out_specs=out_specs, check_vma=False)
```
